256 devices in a mesh: mom: 8 (over z_lo, x), pts: 32 (over y, z_hi, core).
Axes of the slice: x: 4, y: 4, z: 8 (z_hi: 4, z_lo: 2; z = z_hi * 2 + z_lo), core: 2. Of those that a mesh axis runs over, the one named last changes fastest.
Arguments:
- amplitudes: bfloat16 [2, 2, 1, 256, 64, 128], P(None, None, None, 'mom'), may hold values from -6 to 6
- val_orbitals: bfloat16 [2, 256, 64, 512], P(None, 'mom'), may hold values from -0.25 to 0.25
- cond_orbitals: bfloat16 [2, 256, 512, 128], P(None, 'mom', 'pts'), may hold values from -0.25 to 0.25
- screened: bfloat16 [2, 256, 512, 512], P(None, None, ('pts', 'mom')), may hold values from -12 to 12
- val_energy: float32 [256, 64], P('mom', 'pts'), may hold values from -2 to -0.5
- cond_energy: float32 [256, 128], P('mom'), may hold values from 0.5 to 2
- grid_of_slot: int32 [256], replicated, may hold values from 0 to 255, as said below
- opposite_slot: int32 [256], P('mom'), may hold values from 0 to 255, as said below
Outputs:
- applied: float32 [2, 2, 1, 256, 64, 128], P(None, None, None, 'mom', 'pts')
The draws below stay inside these ranges and needn't reach their ends.
Inputs may be any that keep to these rules, and one draw needn't show every extreme that they name: `grid_of_slot`: a permutation of the grid indices. opposite_slot[s] is the slot whose grid index is 255 - grid_of_slot[s]; it is never s, and s and opposite_slot[s] lie in aligned blocks of 32 slots whose first slots differ by 128.
All inputs are finite; a program needn't handle non-finite values.
Results may differ from the reference program's by a relative error of at most 0.006.
Values may be sent and summed in bfloat16 or wider, within the bound.
A program may use at most 128 MiB of HBM per device.

```python
import math
import jax
import jax.numpy as jnp
from jax import lax

NV = 64
NC = 128
NP = 512
NK = 256
NVEC = 1
KD = 32


def pairing(key):
    half_count = NK // 2
    blocks = half_count // KD
    base_key = jax.random.fold_in(key, 11)
    key_perm, key_flip, key_order = jax.random.split(base_key, 3)
    lower_grid = jax.random.permutation(key_perm, half_count).astype(jnp.int32)
    flip_bits = jax.random.randint(key_flip, (half_count,), 0, 2)
    lower_grid = jnp.where(flip_bits == 1, NK - 1 - lower_grid, lower_grid)
    scores = jax.random.randint(key_order, (blocks, KD), 0, 1 << 20) * KD + jnp.arange(KD, dtype=jnp.int32)[None, :]
    within = jnp.argsort(scores, axis=1, stable=True).astype(jnp.int32)
    partner_low = (jnp.arange(blocks, dtype=jnp.int32)[:, None] * KD + within).reshape(half_count)
    upper_grid = NK - 1 - lower_grid[partner_low]
    grid_index = jnp.concatenate([lower_grid, upper_grid]).astype(jnp.int32)
    upper_slots = half_count + jnp.arange(half_count, dtype=jnp.int32)
    opposite = jnp.zeros((NK,), jnp.int32).at[upper_slots].set(partner_low).at[partner_low].set(upper_slots)
    return (grid_index, opposite)


def draw_grid_of_slot(key, part):
    return pairing(key)[0]


def draw_opposite_slot(key, part):
    return pairing(key)[1]


def levels(rng, extent, shards, least, top_value):
    def one(position, blocks):
        draws = jax.random.uniform(jax.random.fold_in(jax.random.fold_in(rng, 6), position), (blocks,), jnp.float32, least / len(shards), top_value / len(shards))
        return jnp.repeat(jnp.exp(draws), extent[position] // blocks).reshape((-1,) + (1,) * (len(extent) - position - 1))

    gain = one(*shards[0])
    for cut in shards[1:]:
        gain = gain * one(*cut)
    return gain


def noise(stream_key, dims, width, reach, cuts=(), kind=jnp.bfloat16):
    drawn = width * jax.random.normal(stream_key, dims, jnp.float32)
    if cuts:
        drawn = drawn * levels(stream_key, dims, cuts, -0.22, 0.18)
    return jnp.clip(drawn, -reach, reach).astype(kind)


def setup_inputs(seed: int = 0) -> dict:
    key_list = jax.random.split(jax.random.key(seed), 9)
    return {
        "amplitudes": noise(key_list[0], (2, 2, NVEC, NK, NV, NC), 1.0, 6.0, ((3, 8),)),
        "val_orbitals": noise(key_list[1], (2, NK, NV, NP), NP ** -0.5, 0.25, ((1, 8),)),
        "cond_orbitals": noise(key_list[2], (2, NK, NP, NC), NP ** -0.5, 0.25, ((1, 8), (2, 32))),
        "screened": noise(key_list[3], (2, NK, NP, NP), 2.0, 12.0, ((2, 256),)),
        "val_energy": jnp.clip(-2.0 + 1.5 * jax.random.uniform(key_list[4], (NK, NV), jnp.float32) ** levels(key_list[4], (NK, NV), ((0, 8), (1, 32)), -0.2, 0.2), -2.0, -0.5),
        "cond_energy": jnp.clip(0.5 + 1.5 * jax.random.uniform(key_list[5], (NK, NC), jnp.float32) ** levels(key_list[5], (NK, NC), ((0, 8),), -0.2, 0.2), 0.5, 2.0),
        "grid_of_slot": draw_grid_of_slot(jax.random.fold_in(key_list[8], 71), 0),
        "opposite_slot": draw_opposite_slot(jax.random.fold_in(key_list[8], 71), 0),
    }


def complex_mix(formula, left, right, left_sign, right_sign):
    left_real = left[0].astype(jnp.float32)
    left_imag = left[1].astype(jnp.float32)
    right_real = right[0].astype(jnp.float32)
    right_imag = right[1].astype(jnp.float32)
    high = lax.Precision.HIGHEST
    real_real = jnp.einsum(formula, left_real, right_real, precision=high)
    imag_imag = jnp.einsum(formula, left_imag, right_imag, precision=high)
    real_imag = jnp.einsum(formula, left_real, right_imag, precision=high)
    imag_real = jnp.einsum(formula, left_imag, right_real, precision=high)
    return jnp.stack([real_real - left_sign * right_sign * imag_imag,
                      right_sign * real_imag + left_sign * imag_real])


def reference(amplitudes, val_orbitals, cond_orbitals, screened, val_energy, cond_energy, grid_of_slot, opposite_slot):
    frequency = jnp.arange(NK, dtype=jnp.int32)
    phases = (frequency[:, None] * grid_of_slot[None, :]) % NK
    angles = phases.astype(jnp.float32) * (2.0 * math.pi / NK)
    cosine_table = jnp.cos(angles).astype(jnp.bfloat16)
    sine_table = jnp.sin(angles).astype(jnp.bfloat16)
    nu_block = NP // 8
    fields = jnp.swapaxes(amplitudes.reshape(2, 2 * NVEC, NK, NV, NC), 0, 1)

    def one_field(coefficient):
        def accumulate(running, offset):
            cond_block = lax.dynamic_slice_in_dim(cond_orbitals, offset, nu_block, 2)
            screen_block = lax.dynamic_slice_in_dim(screened, offset, nu_block, 2)
            half_product = complex_mix("kvc,kuc->kvu", coefficient, cond_block, 1.0, 1.0).astype(jnp.bfloat16)
            pair_values = complex_mix("kvu,kvm->kum", half_product, val_orbitals, 1.0, -1.0).astype(jnp.bfloat16)
            flattened = pair_values.reshape(2, NK, nu_block * NP)
            spec_real = (jnp.dot(cosine_table, flattened[0], preferred_element_type=jnp.float32)
                         + jnp.dot(sine_table, flattened[1], preferred_element_type=jnp.float32))
            spec_imag = (jnp.dot(cosine_table, flattened[1], preferred_element_type=jnp.float32)
                         - jnp.dot(sine_table, flattened[0], preferred_element_type=jnp.float32))
            screen_flat = screen_block.reshape(2, NK, nu_block * NP).astype(jnp.float32)
            prod_real = (screen_flat[0] * spec_real - screen_flat[1] * spec_imag).astype(jnp.bfloat16)
            prod_imag = (screen_flat[0] * spec_imag + screen_flat[1] * spec_real).astype(jnp.bfloat16)
            back_real = (jnp.dot(cosine_table.T, prod_real, preferred_element_type=jnp.float32)
                         - jnp.dot(sine_table.T, prod_imag, preferred_element_type=jnp.float32)) * (1.0 / NK)
            back_imag = (jnp.dot(cosine_table.T, prod_imag, preferred_element_type=jnp.float32)
                         + jnp.dot(sine_table.T, prod_real, preferred_element_type=jnp.float32)) * (1.0 / NK)
            field_pts = jnp.stack([back_real, back_imag]).astype(jnp.bfloat16).reshape(2, NK, nu_block, NP)
            weighted = complex_mix("kum,kvm->kvu", field_pts, val_orbitals, 1.0, 1.0).astype(jnp.bfloat16)
            return running + complex_mix("kvu,kuc->kvc", weighted, cond_block, 1.0, -1.0), None

        offsets = jnp.arange(8, dtype=jnp.int32) * nu_block
        start_sum = jnp.zeros((2, NK, NV, NC), jnp.float32)
        result_sum, unused = lax.scan(accumulate, start_sum, offsets)
        return result_sum

    band_values = lax.map(one_field, fields)
    band_values = jnp.swapaxes(band_values, 0, 1).reshape(2, 2, NVEC, NK, NV, NC)
    mirrored = jnp.take(band_values, opposite_slot, axis=3)
    energy_gap = cond_energy[:, None, :] - val_energy[:, :, None]
    own_rows = amplitudes.astype(jnp.float32)
    result_real = energy_gap * own_rows[0, 0] - band_values[0, 0] - mirrored[0, 1]
    result_imag = energy_gap * own_rows[1, 0] - band_values[1, 0] + mirrored[1, 1]
    anti_real = -energy_gap * own_rows[0, 1] + band_values[0, 1] + mirrored[0, 0]
    anti_imag = -energy_gap * own_rows[1, 1] + band_values[1, 1] - mirrored[1, 0]
    return jnp.stack([jnp.stack([result_real, anti_real]), jnp.stack([result_imag, anti_imag])])
```

```python
import math

import jax
import jax.numpy as jnp
from jax import lax
from jax.experimental import pallas as pl
from jax.experimental.pallas import tpu as pltpu
from jax.sharding import PartitionSpec as P

MESH = pl.DeviceIdType.MESH
F32 = jnp.float32
BF16 = jnp.bfloat16
NT = (((1,), (1,)), ((), ()))
TN = (((0,), (0,)), ((), ()))
STEP_A = 4
STEP_D = 4


def dot(a, b, dims=(((1,), (0,)), ((), ()))):
    return lax.dot_general(a, b, dims, preferred_element_type=F32)


def kernel(
    x_hbm, v_hbm, c_hbm, w_hbm, val_e, cond_e, grid_row, opp_row,
    out,
    x, v, c, w, fwd, inv, spread, send1, recv1, send2, recv2, band, own_x,
    send_c, recv_c, own_y, send_y, recv_y, own_z, send_z, recv_z, total, send_p, recv_p,
    load_sem, self_sem, s1, r1, s2, r2, sc, rc, sy, ry, sz, rz, sp, rp,
):
    m = lax.axis_index("mom")
    p = lax.axis_index("pts")
    mx, mz = m % 4, m // 4
    py, ph, pc = p // 8, (p // 2) % 4, p % 2

    def mom_to(j):
        return ((mz + j // 4) % 2) * 4 + (mx + j % 4) % 4

    def mom_from(j):
        return ((mz + j // 4) % 2) * 4 + (mx + 4 - j % 4) % 4

    core_peer = (m, p + 1 - 2 * pc)

    def y_to(d):
        return (m, ((py + d) % 4) * 8 + p % 8)

    def z_to(d):
        return (m, py * 8 + ((ph + d) % 4) * 2 + pc)

    swap_peer = ((m + 4) % 8, p)

    barrier = pltpu.get_barrier_semaphore()
    peers = [(mom_to(j), p) for j in range(1, 8)] + [core_peer]
    peers += [y_to(d) for d in range(1, 4)] + [z_to(d) for d in range(1, 4)]
    for peer in peers:
        pl.semaphore_signal(barrier, inc=1, device_id=peer, device_id_type=MESH)

    loads = [pltpu.make_async_copy(c_hbm, c, load_sem.at[0])]
    for h in range(2):
        rows = pl.ds(16 * h, 16)
        loads.append(pltpu.make_async_copy(x_hbm.at[:, :, rows], x.at[:, :, rows], load_sem.at[1 + 2 * h]))
        loads.append(pltpu.make_async_copy(v_hbm.at[:, rows], v.at[:, rows], load_sem.at[2 + 2 * h]))
    loads.append(pltpu.make_async_copy(w_hbm, w, load_sem.at[5]))
    for load in loads:
        load.start()

    lane = lax.broadcasted_iota(jnp.int32, (16, 128), 1)
    sign = jnp.where(lane < 64, -1.0, 1.0).astype(F32)

    def pair_step(i, carry):
        ks = [i * STEP_A + u for u in range(STEP_A)]
        halves = []
        for k in ks:
            xk = jnp.concatenate([x[0, 0, k], x[1, 0, k], x[0, 1, k], x[1, 1, k]], axis=0)
            ck = jnp.concatenate([c[0, k], c[1, k]], axis=0)
            halves.append(dot(ck, xk, NT))
        lefts = []
        for h in halves:
            parts = []
            for b in range(2):
                cols = h[:, 128 * b : 128 * (b + 1)]
                q = cols[:16] + sign * pltpu.roll(cols[16:], 64, 1)
                parts += [q, pltpu.roll(q, 64, 1) * -sign]
            lefts.append(jnp.concatenate(parts, axis=0).astype(BF16))
        for k, left in zip(ks, lefts):
            vk = jnp.concatenate([v[0, k], v[1, k]], axis=0)
            pair = dot(left, vk)
            for q in range(4):
                spread.at[q][pl.ds(k, 64, stride=32), :] = pair[:, 128 * q : 128 * (q + 1)]
        return carry

    def pack_pairs(b, h):
        def step(nu, carry):
            for ri in range(2):
                start = pl.multiple_of((b * 32 + ri * 16 + nu) * 32 + 16 * h, 16)
                for q in range(4):
                    send1[b, nu, ri, pl.ds(16 * h, 16), 128 * q : 128 * (q + 1)] = spread[
                        q, pl.ds(start, 16), :
                    ].astype(BF16)
            return carry

        lax.fori_loop(0, 16, step, 0)

    def first_copy(b, h, j, src_m, dst_m, peer):
        i = (b * 2 + h) * 8 + j
        return pltpu.make_async_remote_copy(
            src_ref=send1.at[b, pl.ds(2 * dst_m, 2), :, pl.ds(16 * h, 16), :],
            dst_ref=recv1.at[b, :, :, pl.ds(pl.multiple_of(32 * src_m + 16 * h, 16), 16), :],
            send_sem=s1.at[i],
            recv_sem=r1.at[i],
            device_id=(peer, p),
            device_id_type=MESH,
        )

    firsts = []
    selfs = []
    for h in range(2):
        if h == 0:
            loads[0].wait()
        loads[1 + 2 * h].wait()
        loads[2 + 2 * h].wait()
        lax.fori_loop(h * (16 // STEP_A), (h + 1) * (16 // STEP_A), pair_step, 0)
        if h == 0:
            pl.semaphore_wait(barrier, len(peers))
        for b in range(2):
            pack_pairs(b, h)
            for j in (2, 6, 1, 5, 3, 7, 4):
                copy = first_copy(b, h, j, m, mom_to(j), mom_to(j))
                copy.start()
                firsts.append(copy)
            copy = pltpu.make_async_copy(
                send1.at[b, pl.ds(2 * m, 2), :, pl.ds(16 * h, 16), :],
                recv1.at[b, :, :, pl.ds(pl.multiple_of(32 * m + 16 * h, 16), 16), :],
                self_sem.at[b * 2 + h],
            )
            copy.start()
            selfs.append((b, copy))

    frequency = lax.broadcasted_iota(jnp.int32, (256, 256), 0)
    angle = ((frequency * grid_row[...]) & 255).astype(F32) * (2.0 * math.pi / 256)
    cosine = jnp.cos(angle)
    sine = jnp.sin(angle)
    cosine_t = cosine.T
    sine_t = sine.T
    fwd[:256, :256] = cosine.astype(BF16)
    fwd[:256, 256:] = sine.astype(BF16)
    fwd[256:, :256] = (-sine).astype(BF16)
    fwd[256:, 256:] = cosine.astype(BF16)
    scale = 1.0 / 256
    inv[:256, :256] = (cosine_t * scale).astype(BF16)
    inv[:256, 256:] = (sine_t * -scale).astype(BF16)
    inv[256:, :256] = (sine_t * scale).astype(BF16)
    inv[256:, 256:] = (cosine_t * scale).astype(BF16)

    first_row = pl.multiple_of((p // 8) * 16, 16)
    for ri in range(2):
        for b in range(2):
            piece = x[ri, b, :, pl.ds(first_row, 16), :].astype(F32)
            own_x[pl.ds((ri * 2 + b) * 512, 512), :] = piece.reshape(512, 128)
    loads[5].wait()

    def second_copy(b, nu, j, src_m, dst_m, peer):
        i = (b * 2 + nu) * 8 + j
        return pltpu.make_async_remote_copy(
            src_ref=send2.at[b, nu, :, pl.ds(pl.multiple_of(32 * dst_m, 32), 32), :],
            dst_ref=recv2.at[b, 2 * src_m + nu],
            send_sem=s2.at[i],
            recv_sem=r2.at[i],
            device_id=(peer, p),
            device_id_type=MESH,
        )

    seconds = []
    for b in range(2):
        for owner, copy in selfs:
            if owner == b:
                copy.wait()
        for h in range(2):
            for j in range(1, 8):
                first_copy(b, h, j, mom_from(j), m, mom_to(j)).wait_recv()
        for nu in range(2):

            def transform(i, carry, b=b, nu=nu):
                cols = pl.ds(pl.multiple_of(i * 256, 256), 256)
                spec = dot(fwd[...], recv1[b, nu, :, :, cols].reshape(512, 256))
                real, imag = spec[:256], spec[256:]
                wr = w[nu, 0, :, cols].astype(F32)
                wi = w[nu, 1, :, cols].astype(F32)
                prod = jnp.concatenate([wr * real - wi * imag, wr * imag + wi * real], axis=0)
                back = dot(inv[...], prod.astype(BF16))
                send2[b, nu, :, :, cols] = back.astype(BF16).reshape(2, 256, 256)
                return carry

            lax.fori_loop(0, 2, transform, 0)
            for j in (2, 6, 1, 5, 3, 7, 4):
                copy = second_copy(b, nu, j, m, mom_to(j), mom_to(j))
                copy.start()
                seconds.append(copy)
            copy = pltpu.make_async_copy(
                send2.at[b, nu, :, pl.ds(pl.multiple_of(32 * m, 32), 32), :],
                recv2.at[b, 2 * m + nu],
                self_sem.at[4 + b * 2 + nu],
            )
            copy.start()
            selfs.append((2 + b, copy))

    def band_step(b):
        def step(i, carry):
            ks = [i * STEP_D + u for u in range(STEP_D)]
            mixed = []
            for k in ks:
                left = jnp.concatenate(
                    [spread.at[q][pl.ds(b * 1024 + k, 32, stride=32), :] for q in range(4)], axis=1
                ).astype(BF16)
                vk = jnp.concatenate([v[0, k], v[1, k]], axis=0)
                mixed.append(dot(left, vk, NT))
            lefts = []
            for o in mixed:
                q = o[:16] + sign * pltpu.roll(o[16:], 64, 1)
                lefts.append(jnp.concatenate([q, pltpu.roll(q, 64, 1) * -sign], axis=0).astype(BF16))
            for k, left in zip(ks, lefts):
                ck = jnp.concatenate([c[0, k], c[1, k]], axis=0)
                band.at[b][pl.ds(k, 128, stride=32), :] = dot(left, ck, TN)
            return carry

        return step

    def piece_rows(ri, y, z, core):
        return pl.ds(pl.multiple_of(((ri * 4 + y) * 4 + z) * 128 + core * 64, 64), 64)

    def remote(src, dst, send, recv, peer):
        return pltpu.make_async_remote_copy(
            src_ref=src, dst_ref=dst, send_sem=send, recv_sem=recv, device_id=peer, device_id_type=MESH
        )

    swaps = []
    later = []
    for b in range(2):
        for owner, copy in selfs:
            if owner == 2 + b:
                copy.wait()
        for nu in range(2):
            for j in range(1, 8):
                second_copy(b, nu, j, mom_from(j), m, mom_to(j)).wait_recv()

        def unpack(nu, carry, b=b):
            for ri in range(2):
                start = pl.multiple_of(b * 1024 + (ri * 16 + nu) * 32, 32)
                for q in range(4):
                    spread[q, pl.ds(start, 32), :] = recv2[
                        b, nu, ri, :, 128 * q : 128 * (q + 1)
                    ].astype(F32)
            return carry

        lax.fori_loop(0, 16, unpack, 0)
        lax.fori_loop(0, 32 // STEP_D, band_step(b), 0)

        for ri in range(2):
            for y in range(4):
                for z in range(4):
                    send_c[b, ri, y, z] = band[b, piece_rows(ri, y, z, 1 - pc), :].astype(BF16)
        core_copy = remote(send_c.at[b], recv_c.at[b], sc.at[b], rc.at[b], core_peer)
        core_copy.start()
        core_copy.wait_recv()
        later.append(core_copy)
        y_copies = []
        for d in (2, 1, 3, 0):
            yy = (py + d) % 4
            for ri in range(2):
                for z in range(4):
                    part = band[b, piece_rows(ri, yy, z, pc), :] + recv_c[b, ri, yy, z].astype(F32)
                    if d == 0:
                        own_y[ri, z] = part
                    else:
                        send_y[b, d - 1, ri, z] = part.astype(BF16)
            if d:
                copy = remote(
                    send_y.at[b, d - 1], recv_y.at[b, d - 1], sy.at[b * 3 + d - 1], ry.at[b * 3 + d - 1], y_to(d)
                )
                copy.start()
                y_copies.append(copy)
        for copy in y_copies:
            copy.wait_recv()
        later += y_copies
        z_copies = []
        for d in (2, 1, 3, 0):
            zz = (ph + d) % 4
            for ri in range(2):
                part = own_y[ri, zz]
                for i in range(3):
                    part += recv_y[b, i, ri, zz].astype(F32)
                if d == 0:
                    own_z[ri] = part
                else:
                    send_z[b, d - 1, ri] = part.astype(BF16)
            if d:
                copy = remote(
                    send_z.at[b, d - 1], recv_z.at[b, d - 1], sz.at[b * 3 + d - 1], rz.at[b * 3 + d - 1], z_to(d)
                )
                copy.start()
                z_copies.append(copy)
        for copy in z_copies:
            copy.wait_recv()
        later += z_copies
        for ri in range(2):
            part = own_z[ri]
            for i in range(3):
                part += recv_z[b, i, ri].astype(F32)
            total[b, ri] = part
            send_p[b, ri] = part.astype(BF16)
        swap = remote(send_p.at[b], recv_p.at[b], sp.at[b], rp.at[b], swap_peer)
        swap.start()
        swaps.append(swap)

    slot = lax.broadcasted_iota(jnp.int32, (32, 32), 0)
    pick = jnp.where(slot == (opp_row[...] & 31), 1.0, 0.0).astype(BF16)
    across = lax.broadcasted_iota(jnp.int32, (32, 32), 1)
    for swap in swaps:
        swap.wait_recv()
    for row in range(2):
        energy = jnp.sum(jnp.where(slot == across, val_e[row : row + 1, :], 0.0), axis=1, keepdims=True)
        gap = cond_e[...] - energy
        rows = pl.ds(row * 32, 32)
        for b in range(2):
            for ri in range(2):
                own = own_x[pl.ds((ri * 2 + b) * 512 + 2 * (p % 8) + row, 32, stride=16), :]
                mirrored = dot(pick, recv_p[1 - b, ri, rows, :], TN)
                here = total[b, ri, rows, :]
                turned = mirrored if ri == 0 else -mirrored
                result = gap * own - here - turned
                if b == 1:
                    result = -gap * own + here + turned
                out[pl.ds((ri * 2 + b) * 64 + row, 32, stride=2), :] = result

    for copy in firsts + seconds + later + swaps:
        copy.wait_send()


def on_device(
    amplitudes, val_orbitals, cond_orbitals, screened, val_energy, cond_energy, grid_of_slot, opposite_slot
):
    weights = jnp.transpose(screened, (2, 0, 1, 3))
    hbm = pl.BlockSpec(memory_space=pl.ANY)
    vmem = pl.BlockSpec(memory_space=pltpu.VMEM)
    dma = pltpu.SemaphoreType.DMA
    out = pl.pallas_call(
        kernel,
        out_shape=jax.ShapeDtypeStruct((256, 128), F32),
        in_specs=[hbm] * 4 + [vmem] * 4,
        out_specs=vmem,
        scratch_shapes=[
            pltpu.VMEM((2, 2, 32, 64, 128), BF16),
            pltpu.VMEM((2, 32, 64, 512), BF16),
            pltpu.VMEM((2, 32, 16, 128), BF16),
            pltpu.VMEM((2, 2, 256, 512), BF16),
            pltpu.VMEM((512, 512), BF16),
            pltpu.VMEM((512, 512), BF16),
            pltpu.VMEM((4, 2048, 128), F32),
            pltpu.VMEM((2, 16, 2, 32, 512), BF16),
            pltpu.VMEM((2, 2, 2, 256, 512), BF16),
            pltpu.VMEM((2, 2, 2, 256, 512), BF16),
            pltpu.VMEM((2, 16, 2, 32, 512), BF16),
            pltpu.VMEM((2, 4096, 128), F32),
            pltpu.VMEM((2048, 128), F32),
            pltpu.VMEM((2, 2, 4, 4, 64, 128), BF16),
            pltpu.VMEM((2, 2, 4, 4, 64, 128), BF16),
            pltpu.VMEM((2, 4, 64, 128), F32),
            pltpu.VMEM((2, 3, 2, 4, 64, 128), BF16),
            pltpu.VMEM((2, 3, 2, 4, 64, 128), BF16),
            pltpu.VMEM((2, 64, 128), F32),
            pltpu.VMEM((2, 3, 2, 64, 128), BF16),
            pltpu.VMEM((2, 3, 2, 64, 128), BF16),
            pltpu.VMEM((2, 2, 64, 128), F32),
            pltpu.VMEM((2, 2, 64, 128), BF16),
            pltpu.VMEM((2, 2, 64, 128), BF16),
            dma((6,)), dma((8,)), dma((32,)), dma((32,)), dma((32,)), dma((32,)),
            dma((2,)), dma((2,)), dma((6,)), dma((6,)), dma((6,)), dma((6,)), dma((2,)), dma((2,)),
        ],
        compiler_params=pltpu.CompilerParams(
            collective_id=0, has_side_effects=True, vmem_limit_bytes=56 * 2**20
        ),
        cost_estimate=pl.CostEstimate(flops=2800000000, bytes_accessed=8000000, transcendentals=131072),
    )(
        amplitudes.reshape(2, 2, 32, 64, 128),
        val_orbitals,
        cond_orbitals,
        weights,
        val_energy.T,
        cond_energy,
        grid_of_slot.reshape(1, 256),
        opposite_slot.reshape(1, 32),
    )
    return out.reshape(2, 2, 1, 32, 2, 128)


def solution(mesh):
    in_specs = (
        P(None, None, None, "mom", None, None),
        P(None, "mom", None, None),
        P(None, "mom", "pts", None),
        P(None, None, ("pts", "mom"), None),
        P("mom", "pts"),
        P("mom", None),
        P(),
        P("mom"),
    )
    out_specs = P(None, None, None, "mom", "pts", None)
    return jax.shard_map(
        on_device, mesh=mesh, in_specs=in_specs, out_specs=out_specs, check_vma=False
    )
```

```python
import math

import jax
import jax.numpy as jnp
from jax import lax
from jax.experimental import pallas as pl
from jax.experimental.pallas import tpu as pltpu
from jax.sharding import PartitionSpec as P

MESH = pl.DeviceIdType.MESH
F32 = jnp.float32
BF16 = jnp.bfloat16
NT = (((1,), (1,)), ((), ()))
TN = (((0,), (0,)), ((), ()))
ORDER = (2, 6, 1, 5, 3, 7, 4)


def dot(a, b, dims=(((1,), (0,)), ((), ()))):
    return lax.dot_general(a, b, dims, preferred_element_type=F32)


def aligned(value, by):
    return pl.multiple_of(value, by)


def kernel(
    x_hbm, v_hbm, c_hbm, w_hbm, val_e, cond_e, grid_row, opp_row,
    out,
    x, v, c, c_both, w, w32, fwd, inv, spread, send1, recv1, send2, recv2, band, own_x,
    send_y, recv_y, own_z, send_z, recv_z, total, peer_total, send_p, recv_p, full, mirror,
    load_sem, self_sem, s0, r0, s1, r1, s2, r2, sy, ry, sz, rz, sp, rp, st, rt,
):
    m = lax.axis_index("mom")
    p = lax.axis_index("pts")
    mx, mz = m % 4, m // 4
    py, ph, pc = p // 8, (p // 2) % 4, p % 2
    p_other = p + 1 - 2 * pc

    def mom_to(j):
        return ((mz + j // 4) % 2) * 4 + (mx + j % 4) % 4

    def mom_from(j):
        return ((mz + j // 4) % 2) * 4 + (mx + 4 - j % 4) % 4

    def pts_of(e):
        return p_other if e else p

    def core_of(e):
        return 1 - pc if e else pc

    def y_to(d):
        return (m, ((py + d) % 4) * 8 + p % 8)

    def z_to(d):
        return (m, py * 8 + ((ph + d) % 4) * 2 + pc)

    def remote(src, dst, send, recv, peer):
        return pltpu.make_async_remote_copy(
            src_ref=src, dst_ref=dst, send_sem=send, recv_sem=recv, device_id=peer, device_id_type=MESH
        )

    def load_x(ch):
        rows = pl.ds(8 * ch, 8)
        return pltpu.make_async_copy(x_hbm.at[:, :, rows], x.at[:, :, rows], load_sem.at[ch])

    def load_v(ch):
        rows = pl.ds(8 * ch, 8)
        return pltpu.make_async_copy(v_hbm.at[:, rows], v.at[:, rows], load_sem.at[4 + ch])

    load_c = pltpu.make_async_copy(c_hbm, c, load_sem.at[8])
    load_w = pltpu.make_async_copy(w_hbm, w, load_sem.at[9])
    load_c.start()
    for ch in range(4):
        load_x(ch).start()
        load_v(ch).start()
    load_w.start()

    barrier = pltpu.get_barrier_semaphore()
    peers = [(mom_to(j), pts_of(e)) for j in range(8) for e in range(2) if j + e]
    peers += [y_to(d) for d in range(1, 4)] + [z_to(d) for d in range(1, 4)]
    for peer in peers:
        pl.semaphore_signal(barrier, inc=1, device_id=peer, device_id_type=MESH)

    lane = lax.broadcasted_iota(jnp.int32, (32, 128), 1)
    sign = jnp.where(lane < 64, -1.0, 1.0).astype(F32)

    def first_copy(b, ch, j, src_m, dst_m, peer):
        i = (b * 4 + ch) * 8 + j
        return remote(
            send1.at[b, ch, pl.ds(2 * dst_m, 2)],
            recv1.at[b, :, pl.ds(aligned((src_m * 4 + ch) * 16, 16), 16), :],
            s1.at[i],
            r1.at[i],
            (peer, p),
        )

    def first_self(b, ch):
        return pltpu.make_async_copy(
            send1.at[b, ch, pl.ds(2 * m, 2)],
            recv1.at[b, :, pl.ds(aligned((m * 4 + ch) * 16, 16), 16), :],
            self_sem.at[b * 4 + ch],
        )

    def send_first(b, ch):
        for j in ORDER:
            first_copy(b, ch, j, m, mom_to(j), mom_to(j)).start()
        first_self(b, ch).start()

    def pair_chunk(ch, carry):
        load_x(ch).wait()
        load_v(ch).wait()
        for group in range(2):
            ks = [group * 4 + u for u in range(4)]
            halves = []
            for k8 in ks:
                k = ch * 8 + k8
                xk = jnp.concatenate([x[0, 0, k], x[1, 0, k], x[0, 1, k], x[1, 1, k]], axis=0)
                ck = jnp.concatenate([c[0, k], c[1, k]], axis=0)
                halves.append(dot(ck, xk, NT))
            lefts = []
            for h in halves:
                parts = []
                for b in range(2):
                    cols = h[:, 128 * b : 128 * (b + 1)]
                    q = cols[:16] + sign[:16] * pltpu.roll(cols[16:], 64, 1)
                    parts += [q, pltpu.roll(q, 64, 1) * -sign[:16]]
                lefts.append(jnp.concatenate(parts, axis=0).astype(BF16))
            for k8, left in zip(ks, lefts):
                k = ch * 8 + k8
                pair = dot(left, jnp.concatenate([v[0, k], v[1, k]], axis=0))
                for b in range(2):
                    for ri in range(2):
                        top = (b * 2 + ri) * 16
                        for q in range(4):
                            spread.at[q][pl.ds(b * 256 + ri * 8 + k8, 16, stride=16), :] = pair[
                                top : top + 16, 128 * q : 128 * (q + 1)
                            ]
        for b in range(2):
            for q in range(4):
                send1[b, ch, :, :, 128 * q : 128 * (q + 1)] = (
                    spread[q, 256 * b : 256 * (b + 1), :].astype(BF16).reshape(16, 16, 128)
                )
        send_first(0, ch)
        return carry

    load_c.wait()
    pl.semaphore_wait(barrier, len(peers))
    half = pl.ds(16 * (1 - pc), 16)
    points = pl.ds(aligned(16 * pc, 16), 16)
    points_other = pl.ds(aligned(16 * (1 - pc), 16), 16)
    share_c = remote(c.at[:, half], c_both.at[:, :, points], s0, r0, (m, p_other))
    share_c.start()
    lax.fori_loop(0, 4, pair_chunk, 0)
    c_both[:, :, points] = c[:, pl.ds(16 * pc, 16)]

    def make_tables():
        frequency = lax.broadcasted_iota(jnp.int32, (256, 256), 0)
        angle = ((frequency * grid_row[...]) & 255).astype(F32) * (2.0 * math.pi / 256)
        slot = lax.broadcasted_iota(jnp.int32, (256, 512), 0)
        column = lax.broadcasted_iota(jnp.int32, (256, 512), 1)
        place = jnp.where(slot == (column >> 4) * 8 + (column & 7), 1.0, 0.0).astype(BF16)
        cosine = dot(jnp.cos(angle).astype(BF16), place)
        sine = dot(jnp.sin(angle).astype(BF16), place)
        real = (column & 8) == 0
        top = jnp.where(real, cosine, sine)
        bottom = jnp.where(real, -sine, cosine)
        fwd[:256, :] = top.astype(BF16)
        fwd[256:, :] = bottom.astype(BF16)
        inv[:, :256] = (top.T * (1.0 / 256)).astype(BF16)
        inv[:, 256:] = (bottom.T * (1.0 / 256)).astype(BF16)

    make_tables()
    first_row = aligned((p // 8) * 16, 16)
    for ri in range(2):
        for b in range(2):
            piece = x[ri, b, :, pl.ds(first_row, 16), :].astype(F32)
            own_x[pl.ds((ri * 2 + b) * 512, 512), :] = piece.reshape(512, 128)
    load_w.wait()
    w32[...] = w[...].astype(F32)

    def second_copy(b, kk, j, e, src_m, src_c, dst_m, dst_c, peer):
        i = ((b * 2 + kk) * 8 + j) * 2 + e
        return remote(
            send2.at[b, :, pl.ds(aligned(((dst_m * 2 + dst_c) * 2 + kk) * 16, 16), 16), :],
            recv2.at[b, kk, pl.ds(16 * src_c + 2 * src_m, 2)],
            s2.at[i],
            r2.at[i],
            peer,
        )

    def second_to(b, kk, j, e):
        return second_copy(b, kk, j, e, m, pc, mom_to(j), core_of(e), (mom_to(j), pts_of(e)))

    def second_from(b, kk, j, e):
        return second_copy(b, kk, j, e, mom_from(j), core_of(e), m, pc, (mom_to(j), pts_of(e)))

    def second_self(b, kk):
        return pltpu.make_async_copy(
            send2.at[b, :, pl.ds(aligned(((m * 2 + pc) * 2 + kk) * 16, 16), 16), :],
            recv2.at[b, kk, pl.ds(16 * pc + 2 * m, 2)],
            self_sem.at[8 + b * 2 + kk],
        )

    def send_second(b, kk):
        for j in ORDER + (0,):
            for e in range(2):
                if j + e:
                    second_to(b, kk, j, e).start()
        second_self(b, kk).start()

    def second_sent(b, kk):
        for j in ORDER + (0,):
            for e in range(2):
                if j + e:
                    second_to(b, kk, j, e).wait_send()

    def first_sent(b, ch):
        for j in ORDER:
            first_copy(b, ch, j, m, mom_to(j), mom_to(j)).wait_send()

    def first_arrived(b):
        def step(ch, carry):
            for j in range(1, 8):
                first_copy(b, ch, j, mom_from(j), m, mom_to(j)).wait_recv()
            first_self(b, ch).wait()
            return carry

        lax.fori_loop(0, 4, step, 0)

    def transform_block(b):
        def transform(i, carry):
            nu, half = i // 2, i % 2
            cols = pl.ds(aligned(half * 256, 256), 256)
            spec = dot(fwd[...], recv1[b, nu, :, cols])
            real, imag = spec[:256], spec[256:]

            def weight(ri):
                return jnp.concatenate(
                    [w32[pl.ds(ri * 2048 + (2 * half + t) * 2 + nu, 256, stride=8), :] for t in range(2)], axis=1
                )

            wr, wi = weight(0), weight(1)
            prod = jnp.concatenate([wr * real - wi * imag, wr * imag + wi * real], axis=0)
            send2[b, nu, :, cols] = dot(inv[...], prod.astype(BF16)).astype(BF16)
            return carry

        lax.fori_loop(0, 4, transform, 0)

    def resend(ch, carry):
        first_sent(0, ch)
        send_first(1, ch)
        return carry

    lax.fori_loop(0, 4, resend, 0)
    first_arrived(0)
    transform_block(0)
    first_sent(1, 0)
    first_sent(1, 1)
    send_second(0, 0)
    first_sent(1, 2)
    first_sent(1, 3)
    send_second(0, 1)
    first_arrived(1)
    transform_block(1)
    second_sent(0, 0)
    send_second(1, 0)
    share_c.wait_send()
    remote(c.at[:, half], c_both.at[:, :, points_other], s0, r0, (m, p_other)).wait_recv()

    def second_arrived(b, kk):
        for j in range(8):
            for e in range(2):
                if j + e:
                    second_from(b, kk, j, e).wait_recv()
        second_self(b, kk).wait()

    def band_unit(b, kk):
        for q in range(4):
            spread[q] = recv2[b, kk, :, :, 128 * q : 128 * (q + 1)].astype(F32).reshape(512, 128)
        mixed = []
        for k8 in range(8):
            rows = [
                jnp.concatenate(
                    [spread.at[q][pl.ds(ri * 8 + k8, 32, stride=16), :] for q in range(4)], axis=1
                )
                for ri in range(2)
            ]
            k = 16 * pc + 8 * kk + k8
            vk = jnp.concatenate([v[0, k], v[1, k]], axis=0)
            mixed.append(dot(jnp.concatenate(rows, axis=0).astype(BF16), vk, NT))
        lefts = []
        for o in mixed:
            q = o[:32] + sign * pltpu.roll(o[32:], 64, 1)
            lefts.append(jnp.concatenate([q, pltpu.roll(q, 64, 1) * -sign], axis=0).astype(BF16))
        for k8, left in enumerate(lefts):
            ck = jnp.concatenate([c_both[0, 8 * kk + k8], c_both[1, 8 * kk + k8]], axis=0)
            band.at[b * 2 + kk][pl.ds(k8, 128, stride=8), :] = dot(left, ck, TN)

    def y_copy(u, d):
        i = u * 3 + d - 1
        return remote(send_y.at[u, d - 1], recv_y.at[u, d - 1], sy.at[i], ry.at[i], y_to(d))

    def z_copy(u, d):
        i = u * 3 + d - 1
        return remote(send_z.at[u, d - 1], recv_z.at[u, d - 1], sz.at[i], rz.at[i], z_to(d))

    def y_start(u):
        for d in (2, 1, 3):
            for ri in range(2):
                row = aligned(ri * 512 + ((py + d) % 4) * 128, 128)
                send_y[u, d - 1, ri] = band[u, pl.ds(row, 128), :].astype(BF16)
            y_copy(u, d).start()

    def z_start(u):
        for d in range(1, 4):
            y_copy(u, d).wait_recv()
        for d in (2, 1, 3, 0):
            zz = aligned(((ph + d) % 4) * 32, 32)
            for ri in range(2):
                part = band[u, pl.ds(aligned(ri * 512 + py * 128 + zz, 32), 32), :]
                for i in range(3):
                    part += recv_y[u, i, ri, pl.ds(zz, 32), :].astype(F32)
                if d == 0:
                    own_z[u, ri] = part
                else:
                    send_z[u, d - 1, ri] = part.astype(BF16)
            if d:
                z_copy(u, d).start()

    def finish(u):
        for d in range(1, 4):
            z_copy(u, d).wait_recv()
        b, kk = u // 2, u % 2
        for ri in range(2):
            part = own_z[u, ri]
            for i in range(3):
                part += recv_z[u, i, ri].astype(F32)
            total[u, ri] = part.reshape(2, 16, 128)
            for e in range(2):
                send_p[b, e, kk, ri] = total[u, ri, core_of(e)].astype(BF16)

    def swap_from(b, e):
        return remote(
            send_p.at[b, e],
            recv_p.at[b, core_of(e)],
            sp.at[b * 2 + e],
            rp.at[b * 2 + e],
            ((m + 4) % 8, pts_of(e)),
        )

    def core_copy(b):
        return remote(
            total.at[pl.ds(2 * b, 2), :, 1 - pc], peer_total.at[pl.ds(2 * b, 2)], st.at[b], rt.at[b], (m, p_other)
        )

    def swap_start(b):
        for e in range(2):
            remote(
                send_p.at[b, e], recv_p.at[b, pc], sp.at[b * 2 + e], rp.at[b * 2 + e], ((m + 4) % 8, pts_of(e))
            ).start()
        core_copy(b).start()

    second_arrived(0, 0)
    band_unit(0, 0)
    y_start(0)
    second_sent(0, 1)
    send_second(1, 1)
    second_arrived(0, 1)
    band_unit(0, 1)
    y_start(1)
    z_start(0)
    second_arrived(1, 0)
    band_unit(1, 0)
    y_start(2)
    z_start(1)
    finish(0)
    second_arrived(1, 1)
    band_unit(1, 1)
    y_start(3)
    z_start(2)
    finish(1)
    swap_start(0)
    z_start(3)
    finish(2)
    finish(3)
    swap_start(1)

    slot = lax.broadcasted_iota(jnp.int32, (32, 32), 0)
    pick = jnp.where(slot == (opp_row[...] & 31), 1.0, 0.0).astype(BF16)
    across = lax.broadcasted_iota(jnp.int32, (32, 32), 1)
    gaps = []
    for row in range(2):
        energy = jnp.sum(jnp.where(slot == across, val_e[row : row + 1, :], 0.0), axis=1, keepdims=True)
        gaps.append(cond_e[...] - energy)
    for b in range(2):
        core_copy(b).wait_recv()
        for e in range(2):
            swap_from(b, e).wait_recv()
        for ri in range(2):
            for kk in range(2):
                for row in range(2):
                    part = slice(8 * row, 8 * row + 8)
                    u = b * 2 + kk
                    full[b, ri, row, pl.ds(aligned(16 * pc + 8 * kk, 8), 8), :] = total[u, ri, pc, part]
                    full[b, ri, row, pl.ds(aligned(16 * (1 - pc) + 8 * kk, 8), 8), :] = peer_total[u, ri, part]
                    for core in range(2):
                        mirror[b, ri, row, 16 * core + 8 * kk : 16 * core + 8 * kk + 8, :] = recv_p[
                            b, core, kk, ri
                        ].astype(F32)[part]
    for row in range(2):
        for b in range(2):
            for ri in range(2):
                own = own_x[pl.ds((ri * 2 + b) * 512 + 2 * (p % 8) + row, 32, stride=16), :]
                mirrored = dot(pick, mirror[1 - b, ri, row].astype(BF16), TN)
                here = full[b, ri, row]
                turned = mirrored if ri == 0 else -mirrored
                result = gaps[row] * own - here - turned
                if b == 1:
                    result = -gaps[row] * own + here + turned
                out[pl.ds((ri * 2 + b) * 64 + row, 32, stride=2), :] = result

    second_sent(1, 0)
    second_sent(1, 1)
    for u in range(4):
        for d in range(1, 4):
            y_copy(u, d).wait_send()
            z_copy(u, d).wait_send()
    for b in range(2):
        core_copy(b).wait_send()
        for e in range(2):
            swap_from(b, e).wait_send()


def on_device(
    amplitudes, val_orbitals, cond_orbitals, screened, val_energy, cond_energy, grid_of_slot, opposite_slot
):
    weights = screened.reshape(2, 256, 2, 4, 128).transpose(0, 1, 3, 2, 4).reshape(4096, 128)
    hbm = pl.BlockSpec(memory_space=pl.ANY)
    vmem = pl.BlockSpec(memory_space=pltpu.VMEM)
    dma = pltpu.SemaphoreType.DMA
    out = pl.pallas_call(
        kernel,
        out_shape=jax.ShapeDtypeStruct((256, 128), F32),
        in_specs=[hbm] * 4 + [vmem] * 4,
        out_specs=vmem,
        scratch_shapes=[
            pltpu.VMEM((2, 2, 32, 64, 128), BF16),
            pltpu.VMEM((2, 32, 64, 512), BF16),
            pltpu.VMEM((2, 32, 16, 128), BF16),
            pltpu.VMEM((2, 16, 32, 128), BF16),
            pltpu.VMEM((4096, 128), BF16),
            pltpu.VMEM((4096, 128), F32),
            pltpu.VMEM((512, 512), BF16),
            pltpu.VMEM((512, 512), BF16),
            pltpu.VMEM((4, 512, 128), F32),
            pltpu.VMEM((2, 4, 16, 16, 512), BF16),
            pltpu.VMEM((2, 2, 512, 512), BF16),
            pltpu.VMEM((2, 2, 512, 512), BF16),
            pltpu.VMEM((2, 2, 32, 16, 512), BF16),
            pltpu.VMEM((4, 1024, 128), F32),
            pltpu.VMEM((2048, 128), F32),
            pltpu.VMEM((4, 3, 2, 128, 128), BF16),
            pltpu.VMEM((4, 3, 2, 128, 128), BF16),
            pltpu.VMEM((4, 2, 32, 128), F32),
            pltpu.VMEM((4, 3, 2, 32, 128), BF16),
            pltpu.VMEM((4, 3, 2, 32, 128), BF16),
            pltpu.VMEM((4, 2, 2, 16, 128), F32),
            pltpu.VMEM((4, 2, 16, 128), F32),
            pltpu.VMEM((2, 2, 2, 2, 16, 128), BF16),
            pltpu.VMEM((2, 2, 2, 2, 16, 128), BF16),
            pltpu.VMEM((2, 2, 2, 32, 128), F32),
            pltpu.VMEM((2, 2, 2, 32, 128), F32),
            dma((10,)), dma((12,)), dma, dma, dma((64,)), dma((64,)), dma((64,)), dma((64,)),
            dma((12,)), dma((12,)), dma((12,)), dma((12,)), dma((4,)), dma((4,)), dma((2,)), dma((2,)),
        ],
        compiler_params=pltpu.CompilerParams(
            collective_id=0, has_side_effects=True, vmem_limit_bytes=56 * 2**20
        ),
        cost_estimate=pl.CostEstimate(flops=2800000000, bytes_accessed=8000000, transcendentals=131072),
    )(
        amplitudes.reshape(2, 2, 32, 64, 128),
        val_orbitals,
        cond_orbitals,
        weights,
        val_energy.T,
        cond_energy,
        grid_of_slot.reshape(1, 256),
        opposite_slot.reshape(1, 32),
    )
    return out.reshape(2, 2, 1, 32, 2, 128)


def solution(mesh):
    in_specs = (
        P(None, None, None, "mom", None, None),
        P(None, "mom", None, None),
        P(None, "mom", "pts", None),
        P(None, None, ("pts", "mom"), None),
        P("mom", "pts"),
        P("mom", None),
        P(),
        P("mom"),
    )
    out_specs = P(None, None, None, "mom", "pts", None)
    return jax.shard_map(
        on_device, mesh=mesh, in_specs=in_specs, out_specs=out_specs, check_vma=False
    )
```

```python
import math

import jax
import jax.numpy as jnp
from jax import lax
from jax.experimental import pallas as pl
from jax.experimental.pallas import tpu as pltpu
from jax.sharding import PartitionSpec as P

MESH = pl.DeviceIdType.MESH
F32 = jnp.float32
BF16 = jnp.bfloat16
NT = (((1,), (1,)), ((), ()))
TN = (((0,), (0,)), ((), ()))
ORDER = (2, 6, 1, 5, 3, 7, 4)


def dot(a, b, dims=(((1,), (0,)), ((), ()))):
    return lax.dot_general(a, b, dims, preferred_element_type=F32)


def aligned(value, by):
    return pl.multiple_of(value, by)


def kernel(
    x_hbm, v_hbm, c_hbm, w_hbm, val_e, cond_e, grid_row, opp_row,
    out,
    x, v, c, c_both, w, w32, fwd, inv, spread, send1, recv1, send2, recv2, band, own_x,
    send_y, recv_y, own_z, send_z, recv_z, total, peer_total, send_p, recv_p, full, mirror, own_part,
    load_sem, self_sem, s0, r0, s1, r1, s2, r2, sy, ry, sz, rz, sp, rp, st, rt,
):
    m = lax.axis_index("mom")
    p = lax.axis_index("pts")
    mx, mz = m % 4, m // 4
    py, ph, pc = p // 8, (p // 2) % 4, p % 2
    p_other = p + 1 - 2 * pc

    def mom_to(j):
        return ((mz + j // 4) % 2) * 4 + (mx + j % 4) % 4

    def mom_from(j):
        return ((mz + j // 4) % 2) * 4 + (mx + 4 - j % 4) % 4

    def pts_of(e):
        return p_other if e else p

    def core_of(e):
        return 1 - pc if e else pc

    def y_to(d):
        return (m, ((py + d) % 4) * 8 + p % 8)

    def z_to(d):
        return (m, py * 8 + ((ph + d) % 4) * 2 + pc)

    def remote(src, dst, send, recv, peer):
        return pltpu.make_async_remote_copy(
            src_ref=src, dst_ref=dst, send_sem=send, recv_sem=recv, device_id=peer, device_id_type=MESH
        )

    def load_x(ch):
        rows = pl.ds(8 * ch, 8)
        return pltpu.make_async_copy(x_hbm.at[:, :, rows], x.at[:, :, rows], load_sem.at[ch])

    def load_v(ch):
        rows = pl.ds(8 * ch, 8)
        return pltpu.make_async_copy(v_hbm.at[:, rows], v.at[:, rows], load_sem.at[4 + ch])

    load_c = pltpu.make_async_copy(c_hbm, c, load_sem.at[8])
    load_w = pltpu.make_async_copy(w_hbm, w, load_sem.at[9])
    load_c.start()
    for ch in range(4):
        load_x(ch).start()
        load_v(ch).start()
    load_w.start()

    barrier = pltpu.get_barrier_semaphore()
    peers = [(mom_to(j), pts_of(e)) for j in range(8) for e in range(2) if j + e]
    peers += [y_to(d) for d in range(1, 4)] + [z_to(d) for d in range(1, 4)]
    for peer in peers:
        pl.semaphore_signal(barrier, inc=1, device_id=peer, device_id_type=MESH)

    lane = lax.broadcasted_iota(jnp.int32, (32, 128), 1)
    sign = jnp.where(lane < 64, -1.0, 1.0).astype(F32)

    def first_copy(b, ch, j, src_m, dst_m, peer):
        i = (b * 4 + ch) * 8 + j
        return remote(
            send1.at[b, ch, pl.ds(2 * dst_m, 2)],
            recv1.at[b, :, pl.ds(aligned((src_m * 4 + ch) * 16, 16), 16), :],
            s1.at[i],
            r1.at[i],
            (peer, p),
        )

    def first_self(b, ch):
        return pltpu.make_async_copy(
            send1.at[b, ch, pl.ds(2 * m, 2)],
            recv1.at[b, :, pl.ds(aligned((m * 4 + ch) * 16, 16), 16), :],
            self_sem.at[b * 4 + ch],
        )

    def send_first(b, ch):
        for j in ORDER:
            first_copy(b, ch, j, m, mom_to(j), mom_to(j)).start()
        first_self(b, ch).start()

    def pair_chunk(ch, carry):
        load_x(ch).wait()
        load_v(ch).wait()
        for group in range(2):
            ks = [group * 4 + u for u in range(4)]
            halves = []
            for k8 in ks:
                k = ch * 8 + k8
                xk = jnp.concatenate([x[0, 0, k], x[1, 0, k], x[0, 1, k], x[1, 1, k]], axis=0)
                ck = jnp.concatenate([c[0, k], c[1, k]], axis=0)
                halves.append(dot(ck, xk, NT))
            lefts = []
            for h in halves:
                parts = []
                for b in range(2):
                    cols = h[:, 128 * b : 128 * (b + 1)]
                    q = cols[:16] + sign[:16] * pltpu.roll(cols[16:], 64, 1)
                    parts += [q, pltpu.roll(q, 64, 1) * -sign[:16]]
                lefts.append(jnp.concatenate(parts, axis=0).astype(BF16))
            for k8, left in zip(ks, lefts):
                k = ch * 8 + k8
                pair = dot(left, jnp.concatenate([v[0, k], v[1, k]], axis=0))
                for b in range(2):
                    for ri in range(2):
                        top = (b * 2 + ri) * 16
                        for q in range(4):
                            spread.at[q][pl.ds(b * 256 + ri * 8 + k8, 16, stride=16), :] = pair[
                                top : top + 16, 128 * q : 128 * (q + 1)
                            ]
        for b in range(2):
            for q in range(4):
                send1[b, ch, :, :, 128 * q : 128 * (q + 1)] = (
                    spread[q, 256 * b : 256 * (b + 1), :].astype(BF16).reshape(16, 16, 128)
                )
        return carry

    def pair_and_send(ch, carry):
        pair_chunk(ch, carry)
        send_first(0, ch)
        return carry

    load_c.wait()
    pair_chunk(0, 0)
    pl.semaphore_wait(barrier, len(peers))
    send_first(0, 0)
    half = pl.ds(16 * (1 - pc), 16)
    points = pl.ds(aligned(16 * pc, 16), 16)
    points_other = pl.ds(aligned(16 * (1 - pc), 16), 16)
    share_c = remote(c.at[:, half], c_both.at[:, :, points], s0, r0, (m, p_other))
    share_c.start()
    lax.fori_loop(1, 4, pair_and_send, 0)
    c_both[:, :, points] = c[:, pl.ds(16 * pc, 16)]

    def make_tables():
        frequency = lax.broadcasted_iota(jnp.int32, (256, 256), 0)
        angle = ((frequency * grid_row[...]) & 255).astype(F32) * (2.0 * math.pi / 256)
        slot = lax.broadcasted_iota(jnp.int32, (256, 512), 0)
        column = lax.broadcasted_iota(jnp.int32, (256, 512), 1)
        place = jnp.where(slot == (column >> 4) * 8 + (column & 7), 1.0, 0.0).astype(BF16)
        cosine = dot(jnp.cos(angle).astype(BF16), place)
        sine = dot(jnp.sin(angle).astype(BF16), place)
        real = (column & 8) == 0
        top = jnp.where(real, cosine, sine)
        bottom = jnp.where(real, -sine, cosine)
        fwd[:256, :] = top.astype(BF16)
        fwd[256:, :] = bottom.astype(BF16)
        inv[:, :256] = (top.T * (1.0 / 256)).astype(BF16)
        inv[:, 256:] = (bottom.T * (1.0 / 256)).astype(BF16)

    make_tables()
    first_row = aligned((p // 8) * 16, 16)
    for ri in range(2):
        for b in range(2):
            piece = x[ri, b, :, pl.ds(first_row, 16), :].astype(F32)
            own_x[pl.ds((ri * 2 + b) * 512, 512), :] = piece.reshape(512, 128)
    load_w.wait()
    w32[...] = w[...].astype(F32)

    def second_copy(b, kk, j, e, src_m, src_c, dst_m, dst_c, peer):
        i = ((b * 2 + kk) * 8 + j) * 2 + e
        return remote(
            send2.at[b, :, pl.ds(aligned(((dst_m * 2 + dst_c) * 2 + kk) * 16, 16), 16), :],
            recv2.at[b, kk, pl.ds(16 * src_c + 2 * src_m, 2)],
            s2.at[i],
            r2.at[i],
            peer,
        )

    def second_to(b, kk, j, e):
        return second_copy(b, kk, j, e, m, pc, mom_to(j), core_of(e), (mom_to(j), pts_of(e)))

    def second_from(b, kk, j, e):
        return second_copy(b, kk, j, e, mom_from(j), core_of(e), m, pc, (mom_to(j), pts_of(e)))

    def second_self(b, kk):
        return pltpu.make_async_copy(
            send2.at[b, :, pl.ds(aligned(((m * 2 + pc) * 2 + kk) * 16, 16), 16), :],
            recv2.at[b, kk, pl.ds(16 * pc + 2 * m, 2)],
            self_sem.at[8 + b * 2 + kk],
        )

    def send_second(b, kk):
        for j in ORDER + (0,):
            for e in range(2):
                if j + e:
                    second_to(b, kk, j, e).start()
        second_self(b, kk).start()

    def second_sent(b, kk):
        for j in ORDER + (0,):
            for e in range(2):
                if j + e:
                    second_to(b, kk, j, e).wait_send()

    def first_sent(b, ch):
        for j in ORDER:
            first_copy(b, ch, j, m, mom_to(j), mom_to(j)).wait_send()

    def first_arrived(b):
        def step(ch, carry):
            for j in range(1, 8):
                first_copy(b, ch, j, mom_from(j), m, mom_to(j)).wait_recv()
            first_self(b, ch).wait()
            return carry

        lax.fori_loop(0, 4, step, 0)

    def transform_block(b):
        def transform(i, carry):
            nu, half = i // 2, i % 2
            cols = pl.ds(aligned(half * 256, 256), 256)
            spec = dot(fwd[...], recv1[b, nu, :, cols])
            real, imag = spec[:256], spec[256:]

            def weight(ri):
                return jnp.concatenate(
                    [w32[pl.ds(ri * 2048 + (2 * half + t) * 2 + nu, 256, stride=8), :] for t in range(2)], axis=1
                )

            wr, wi = weight(0), weight(1)
            prod = jnp.concatenate([wr * real - wi * imag, wr * imag + wi * real], axis=0)
            send2[b, nu, :, cols] = dot(inv[...], prod.astype(BF16)).astype(BF16)
            return carry

        lax.fori_loop(0, 4, transform, 0)

    def resend(ch, carry):
        first_sent(0, ch)
        send_first(1, ch)
        return carry

    lax.fori_loop(0, 4, resend, 0)
    first_arrived(0)
    transform_block(0)
    first_sent(1, 0)
    first_sent(1, 1)
    send_second(0, 0)
    first_sent(1, 2)
    first_sent(1, 3)
    send_second(0, 1)
    first_arrived(1)
    transform_block(1)
    second_sent(0, 0)
    send_second(1, 0)
    share_c.wait_send()
    remote(c.at[:, half], c_both.at[:, :, points_other], s0, r0, (m, p_other)).wait_recv()

    def second_arrived(b, kk):
        for j in range(8):
            for e in range(2):
                if j + e:
                    second_from(b, kk, j, e).wait_recv()
        second_self(b, kk).wait()

    def band_unit(b, kk):
        for q in range(4):
            spread[q] = recv2[b, kk, :, :, 128 * q : 128 * (q + 1)].astype(F32).reshape(512, 128)
        mixed = []
        for k8 in range(8):
            rows = [
                jnp.concatenate(
                    [spread.at[q][pl.ds(ri * 8 + k8, 32, stride=16), :] for q in range(4)], axis=1
                )
                for ri in range(2)
            ]
            k = 16 * pc + 8 * kk + k8
            vk = jnp.concatenate([v[0, k], v[1, k]], axis=0)
            mixed.append(dot(jnp.concatenate(rows, axis=0).astype(BF16), vk, NT))
        lefts = []
        for o in mixed:
            q = o[:32] + sign * pltpu.roll(o[32:], 64, 1)
            lefts.append(jnp.concatenate([q, pltpu.roll(q, 64, 1) * -sign], axis=0).astype(BF16))
        for k8, left in enumerate(lefts):
            ck = jnp.concatenate([c_both[0, 8 * kk + k8], c_both[1, 8 * kk + k8]], axis=0)
            band.at[b * 2 + kk][pl.ds(k8, 128, stride=8), :] = dot(left, ck, TN)

    def y_copy(u, d):
        i = u * 3 + d - 1
        return remote(send_y.at[u, d - 1], recv_y.at[u, d - 1], sy.at[i], ry.at[i], y_to(d))

    def z_copy(u, d):
        i = u * 3 + d - 1
        return remote(send_z.at[u, d - 1], recv_z.at[u, d - 1], sz.at[i], rz.at[i], z_to(d))

    def y_start(u):
        for d in (2, 1, 3):
            for ri in range(2):
                row = aligned(ri * 512 + ((py + d) % 4) * 128, 128)
                send_y[u, d - 1, ri] = band[u, pl.ds(row, 128), :].astype(BF16)
            y_copy(u, d).start()

    def z_start(u):
        for d in range(1, 4):
            y_copy(u, d).wait_recv()
        for d in (2, 1, 3, 0):
            zz = aligned(((ph + d) % 4) * 32, 32)
            for ri in range(2):
                part = band[u, pl.ds(aligned(ri * 512 + py * 128 + zz, 32), 32), :]
                for i in range(3):
                    part += recv_y[u, i, ri, pl.ds(zz, 32), :].astype(F32)
                if d == 0:
                    own_z[u, ri] = part
                else:
                    send_z[u, d - 1, ri] = part.astype(BF16)
            if d:
                z_copy(u, d).start()

    def finish(u):
        for d in range(1, 4):
            z_copy(u, d).wait_recv()
        b, kk = u // 2, u % 2
        for ri in range(2):
            part = own_z[u, ri]
            for i in range(3):
                part += recv_z[u, i, ri].astype(F32)
            total[u, ri] = part.reshape(2, 16, 128)
            for e in range(2):
                send_p[b, e, kk, ri] = total[u, ri, core_of(e)].astype(BF16)

    def swap_from(b, e):
        return remote(
            send_p.at[b, e],
            recv_p.at[b, core_of(e)],
            sp.at[b * 2 + e],
            rp.at[b * 2 + e],
            ((m + 4) % 8, pts_of(e)),
        )

    def core_copy(b):
        return remote(
            total.at[pl.ds(2 * b, 2), :, 1 - pc], peer_total.at[pl.ds(2 * b, 2)], st.at[b], rt.at[b], (m, p_other)
        )

    def swap_start(b):
        for e in range(2):
            remote(
                send_p.at[b, e], recv_p.at[b, pc], sp.at[b * 2 + e], rp.at[b * 2 + e], ((m + 4) % 8, pts_of(e))
            ).start()
        core_copy(b).start()

    def y_sent(u):
        for d in range(1, 4):
            y_copy(u, d).wait_send()

    def z_sent(u):
        for d in range(1, 4):
            z_copy(u, d).wait_send()

    def swap_sent(b):
        core_copy(b).wait_send()
        for e in range(2):
            swap_from(b, e).wait_send()

    def place(b):
        core_copy(b).wait_recv()
        for e in range(2):
            swap_from(b, e).wait_recv()
        for ri in range(2):
            for kk in range(2):
                for row in range(2):
                    part = slice(8 * row, 8 * row + 8)
                    u = b * 2 + kk
                    full[b, ri, row, pl.ds(aligned(16 * pc + 8 * kk, 8), 8), :] = total[u, ri, pc, part]
                    full[b, ri, row, pl.ds(aligned(16 * (1 - pc) + 8 * kk, 8), 8), :] = peer_total[u, ri, part]
                    for core in range(2):
                        mirror[b, ri, row, 16 * core + 8 * kk : 16 * core + 8 * kk + 8, :] = recv_p[
                            b, core, kk, ri
                        ].astype(F32)[part]

    def own_term():
        for row in range(2):
            energy = jnp.sum(jnp.where(slot == across, val_e[row : row + 1, :], 0.0), axis=1, keepdims=True)
            gap = cond_e[...] - energy
            for b in range(2):
                for ri in range(2):
                    rows = pl.ds((ri * 2 + b) * 512 + 2 * (p % 8) + row, 32, stride=16)
                    result = gap * own_x[rows, :]
                    own_part[b, ri, row] = -result if b else result

    def add_mirrored(b):
        for row in range(2):
            for ri in range(2):
                mirrored = dot(pick, mirror[b, ri, row].astype(BF16), TN)
                here = full[b, ri, row]
                down = mirrored if ri == 0 else -mirrored
                own_part[1 - b, ri, row] += -down if b else down
                own_part[b, ri, row] += here if b else -here

    slot = lax.broadcasted_iota(jnp.int32, (32, 32), 0)
    across = lax.broadcasted_iota(jnp.int32, (32, 32), 1)
    pick = jnp.where(slot == (opp_row[...] & 31), 1.0, 0.0).astype(BF16)
    own_term()
    second_arrived(0, 0)
    band_unit(0, 0)
    y_start(0)
    second_sent(0, 1)
    send_second(1, 1)
    second_arrived(0, 1)
    band_unit(0, 1)
    y_start(1)
    z_start(0)
    second_arrived(1, 0)
    band_unit(1, 0)
    y_start(2)
    z_start(1)
    finish(0)
    second_arrived(1, 1)
    band_unit(1, 1)
    y_start(3)
    z_start(2)
    finish(1)
    swap_start(0)
    second_sent(1, 0)
    second_sent(1, 1)
    for u in range(3):
        y_sent(u)
    z_sent(0)
    z_sent(1)
    z_start(3)
    finish(2)
    place(0)
    add_mirrored(0)
    y_sent(3)
    finish(3)
    swap_start(1)
    z_sent(2)
    z_sent(3)
    swap_sent(0)
    place(1)
    add_mirrored(1)
    for row in range(2):
        for b in range(2):
            for ri in range(2):
                out[pl.ds((ri * 2 + b) * 64 + row, 32, stride=2), :] = own_part[b, ri, row]
    swap_sent(1)


def on_device(
    amplitudes, val_orbitals, cond_orbitals, screened, val_energy, cond_energy, grid_of_slot, opposite_slot
):
    weights = screened.reshape(2, 256, 2, 4, 128).transpose(0, 1, 3, 2, 4).reshape(4096, 128)
    hbm = pl.BlockSpec(memory_space=pl.ANY)
    vmem = pl.BlockSpec(memory_space=pltpu.VMEM)
    dma = pltpu.SemaphoreType.DMA
    out = pl.pallas_call(
        kernel,
        out_shape=pltpu.VMEM((256, 128), F32),
        in_specs=[hbm] * 4 + [vmem] * 4,
        out_specs=vmem,
        scratch_shapes=[
            pltpu.VMEM((2, 2, 32, 64, 128), BF16),
            pltpu.VMEM((2, 32, 64, 512), BF16),
            pltpu.VMEM((2, 32, 16, 128), BF16),
            pltpu.VMEM((2, 16, 32, 128), BF16),
            pltpu.VMEM((4096, 128), BF16),
            pltpu.VMEM((4096, 128), F32),
            pltpu.VMEM((512, 512), BF16),
            pltpu.VMEM((512, 512), BF16),
            pltpu.VMEM((4, 512, 128), F32),
            pltpu.VMEM((2, 4, 16, 16, 512), BF16),
            pltpu.VMEM((2, 2, 512, 512), BF16),
            pltpu.VMEM((2, 2, 512, 512), BF16),
            pltpu.VMEM((2, 2, 32, 16, 512), BF16),
            pltpu.VMEM((4, 1024, 128), F32),
            pltpu.VMEM((2048, 128), F32),
            pltpu.VMEM((4, 3, 2, 128, 128), BF16),
            pltpu.VMEM((4, 3, 2, 128, 128), BF16),
            pltpu.VMEM((4, 2, 32, 128), F32),
            pltpu.VMEM((4, 3, 2, 32, 128), BF16),
            pltpu.VMEM((4, 3, 2, 32, 128), BF16),
            pltpu.VMEM((4, 2, 2, 16, 128), F32),
            pltpu.VMEM((4, 2, 16, 128), F32),
            pltpu.VMEM((2, 2, 2, 2, 16, 128), BF16),
            pltpu.VMEM((2, 2, 2, 2, 16, 128), BF16),
            pltpu.VMEM((2, 2, 2, 32, 128), F32),
            pltpu.VMEM((2, 2, 2, 32, 128), F32),
            pltpu.VMEM((2, 2, 2, 32, 128), F32),
            dma((10,)), dma((12,)), dma, dma, dma((64,)), dma((64,)), dma((64,)), dma((64,)),
            dma((12,)), dma((12,)), dma((12,)), dma((12,)), dma((4,)), dma((4,)), dma((2,)), dma((2,)),
        ],
        compiler_params=pltpu.CompilerParams(
            collective_id=0, has_side_effects=True, vmem_limit_bytes=56 * 2**20
        ),
        cost_estimate=pl.CostEstimate(flops=2800000000, bytes_accessed=8000000, transcendentals=131072),
    )(
        amplitudes.reshape(2, 2, 32, 64, 128),
        val_orbitals,
        cond_orbitals,
        weights,
        val_energy.T,
        cond_energy,
        grid_of_slot.reshape(1, 256),
        opposite_slot.reshape(1, 32),
    )
    return out.reshape(2, 2, 1, 32, 2, 128)


def solution(mesh):
    in_specs = (
        P(None, None, None, "mom", None, None),
        P(None, "mom", None, None),
        P(None, "mom", "pts", None),
        P(None, None, ("pts", "mom"), None),
        P("mom", "pts"),
        P("mom", None),
        P(),
        P("mom"),
    )
    out_specs = P(None, None, None, "mom", "pts", None)
    return jax.shard_map(
        on_device, mesh=mesh, in_specs=in_specs, out_specs=out_specs, check_vma=False
    )
```

```python
import math

import jax
import jax.numpy as jnp
from jax import lax
from jax.experimental import pallas as pl
from jax.experimental.pallas import tpu as pltpu
from jax.sharding import PartitionSpec as P

MESH = pl.DeviceIdType.MESH
F32 = jnp.float32
BF16 = jnp.bfloat16
NT = (((1,), (1,)), ((), ()))
TN = (((0,), (0,)), ((), ()))
ORDER = (2, 6, 1, 5, 3, 7, 4)
WIDE = tuple((d, e, t) for d in (2, 1, 3, 0) for t in (1, 0) for e in (0, 1) if d + e + t)
UNITS = ((0, 0, 2), (0, 2, 2), (1, 0, 2), (1, 2, 1), (1, 3, 1))


def dot(a, b, dims=(((1,), (0,)), ((), ()))):
    return lax.dot_general(a, b, dims, preferred_element_type=F32)


def aligned(value, by):
    return pl.multiple_of(value, by)


def kernel(
    x_hbm, v_hbm, c_hbm, w_hbm, val_e, cond_e, grid_row, opp_row,
    out,
    x, v, c, c_both, w, w32, fwd, inv, spread, send1, recv1, send2, recv2, band, own_x,
    send_y, recv_y, own_z, send_z, recv_z, send_w, recv_w, total, peer_total,
    send_p, recv_p, mirror,
    load_sem, self_sem, s0, r0, s1, r1, s2, r2, sy, ry, sz, rz, sw, rw, sp, rp, st, rt,
):
    m = lax.axis_index("mom")
    p = lax.axis_index("pts")
    mx, mz = m % 4, m // 4
    py, ph, pc = p // 8, (p // 2) % 4, p % 2
    p_other = p + 1 - 2 * pc

    def mom_to(j):
        return ((mz + j // 4) % 2) * 4 + (mx + j % 4) % 4

    def mom_from(j):
        return ((mz + j // 4) % 2) * 4 + (mx + 4 - j % 4) % 4

    def pts_of(e):
        return p_other if e else p

    def core_of(e):
        return 1 - pc if e else pc

    def y_to(d):
        return (m, ((py + d) % 4) * 8 + p % 8)

    def z_to(d):
        return (m, py * 8 + ((ph + d) % 4) * 2 + pc)

    def wide_to(d, e, t):
        return ((m + 4 * t) % 8, py * 8 + ((ph + d) % 4) * 2 + core_of(e))

    def remote(src, dst, send, recv, peer):
        return pltpu.make_async_remote_copy(
            src_ref=src, dst_ref=dst, send_sem=send, recv_sem=recv, device_id=peer, device_id_type=MESH
        )

    def load_x(ch):
        rows = pl.ds(8 * ch, 8)
        return pltpu.make_async_copy(x_hbm.at[:, :, rows], x.at[:, :, rows], load_sem.at[ch])

    def load_v(ch):
        rows = pl.ds(8 * ch, 8)
        return pltpu.make_async_copy(v_hbm.at[:, rows], v.at[:, rows], load_sem.at[4 + ch])

    load_c = pltpu.make_async_copy(c_hbm, c, load_sem.at[8])
    load_w = pltpu.make_async_copy(w_hbm, w, load_sem.at[9])
    load_c.start()
    load_x(0).start()
    load_v(0).start()

    barrier = pltpu.get_barrier_semaphore()
    peers = [(mom_to(j), pts_of(e)) for j in range(8) for e in range(2) if j + e]
    peers += [y_to(d) for d in range(1, 4)] + [wide_to(d, e, t) for d, e, t in WIDE if d]
    for peer in peers:
        pl.semaphore_signal(barrier, inc=1, device_id=peer, device_id_type=MESH)

    lane = lax.broadcasted_iota(jnp.int32, (32, 128), 1)
    sign = jnp.where(lane < 64, -1.0, 1.0).astype(F32)

    def first_copy(b, ch, j, src_m, dst_m, peer):
        i = (b * 4 + ch) * 8 + j
        return remote(
            send1.at[b, ch, pl.ds(2 * dst_m, 2)],
            recv1.at[b, :, pl.ds(aligned((src_m * 4 + ch) * 16, 16), 16), :],
            s1.at[i],
            r1.at[i],
            (peer, p),
        )

    def first_self(b, ch):
        return pltpu.make_async_copy(
            send1.at[b, ch, pl.ds(2 * m, 2)],
            recv1.at[b, :, pl.ds(aligned((m * 4 + ch) * 16, 16), 16), :],
            self_sem.at[b * 4 + ch],
        )

    def send_first(b, ch):
        for j in ORDER:
            first_copy(b, ch, j, m, mom_to(j), mom_to(j)).start()
        first_self(b, ch).start()

    def pair_chunk(ch):
        for group in range(2):
            ks = [group * 4 + u for u in range(4)]
            halves = []
            for k8 in ks:
                k = ch * 8 + k8
                xk = jnp.concatenate([x[0, 0, k], x[1, 0, k], x[0, 1, k], x[1, 1, k]], axis=0)
                ck = jnp.concatenate([c[0, k], c[1, k]], axis=0)
                halves.append(dot(ck, xk, NT))
            lefts = []
            for h in halves:
                parts = []
                for b in range(2):
                    cols = h[:, 128 * b : 128 * (b + 1)]
                    q = cols[:16] + sign[:16] * pltpu.roll(cols[16:], 64, 1)
                    parts += [q, pltpu.roll(q, 64, 1) * -sign[:16]]
                lefts.append(jnp.concatenate(parts, axis=0).astype(BF16))
            for k8, left in zip(ks, lefts):
                k = ch * 8 + k8
                pair = dot(left, jnp.concatenate([v[0, k], v[1, k]], axis=0))
                for b in range(2):
                    for ri in range(2):
                        top = (b * 2 + ri) * 16
                        for q in range(4):
                            spread.at[q][pl.ds(b * 256 + ri * 8 + k8, 16, stride=16), :] = pair[
                                top : top + 16, 128 * q : 128 * (q + 1)
                            ]

    def pack(b, ch):
        for q in range(4):
            send1[b, ch, :, :, 128 * q : 128 * (q + 1)] = (
                spread[q, 256 * b : 256 * (b + 1), :].astype(BF16).reshape(16, 16, 128)
            )

    def pair_and_send(ch, carry):
        load_x(ch).wait()
        load_v(ch).wait()
        pair_chunk(ch)
        pack(0, ch)
        send_first(0, ch)
        pack(1, ch)
        return carry

    load_c.wait()
    load_x(0).wait()
    load_v(0).wait()
    for ch in range(1, 4):
        load_x(ch).start()
        load_v(ch).start()
    load_w.start()
    pair_chunk(0)
    pack(0, 0)
    pl.semaphore_wait(barrier, len(peers))
    send_first(0, 0)
    pack(1, 0)
    half = pl.ds(16 * (1 - pc), 16)
    points = pl.ds(aligned(16 * pc, 16), 16)
    points_other = pl.ds(aligned(16 * (1 - pc), 16), 16)
    share_c = remote(c.at[:, half], c_both.at[:, :, points], s0, r0, (m, p_other))
    share_c.start()
    lax.fori_loop(1, 4, pair_and_send, 0)
    c_both[:, :, points] = c[:, pl.ds(16 * pc, 16)]

    def make_tables():
        frequency = lax.broadcasted_iota(jnp.int32, (256, 256), 0)
        angle = ((frequency * grid_row[...]) & 255).astype(F32) * (2.0 * math.pi / 256)
        slot = lax.broadcasted_iota(jnp.int32, (256, 512), 0)
        column = lax.broadcasted_iota(jnp.int32, (256, 512), 1)
        cos_table = jnp.cos(angle).astype(BF16)
        sin_table = jnp.sin(angle).astype(BF16)

        def halves(slots, real):
            place = jnp.where(slot == slots, 1.0, 0.0).astype(BF16)
            cosine, sine = dot(cos_table, place), dot(sin_table, place)
            return jnp.where(real, cosine, sine), jnp.where(real, -sine, cosine)

        top, bottom = halves((column >> 4) * 8 + (column & 7), (column & 8) == 0)
        fwd[:256, :] = top.astype(BF16)
        fwd[256:, :] = bottom.astype(BF16)
        top, bottom = halves((column >> 5) * 16 + ((column >> 3) & 3) * 4 + (column & 3), (column & 4) == 0)
        inv[:, :256] = (top.T * (1.0 / 256)).astype(BF16)
        inv[:, 256:] = (bottom.T * (1.0 / 256)).astype(BF16)

    make_tables()
    first_row = aligned((p // 8) * 16, 16)
    for ri in range(2):
        for b in range(2):
            piece = x[ri, b, :, pl.ds(first_row, 16), :].astype(F32)
            own_x[pl.ds((ri * 2 + b) * 512, 512), :] = piece.reshape(512, 128)
    load_w.wait()
    w32[...] = w[...].astype(F32)

    def second_copy(u, j, e, src_m, src_c, dst_m, dst_c, peer):
        b, q, n = UNITS[u]
        i = (u * 8 + j) * 2 + e
        return remote(
            send2.at[b, dst_m * 2 + dst_c, pl.ds(q, n)],
            recv2.at[b, pl.ds(q, n), src_c * 8 + src_m],
            s2.at[i],
            r2.at[i],
            peer,
        )

    def second_to(u, j, e):
        return second_copy(u, j, e, m, pc, mom_to(j), core_of(e), (mom_to(j), pts_of(e)))

    def second_from(u, j, e):
        return second_copy(u, j, e, mom_from(j), core_of(e), m, pc, (mom_to(j), pts_of(e)))

    def second_self(u):
        b, q, n = UNITS[u]
        return pltpu.make_async_copy(
            send2.at[b, m * 2 + pc, pl.ds(q, n)], recv2.at[b, pl.ds(q, n), pc * 8 + m], self_sem.at[8 + u]
        )

    def send_second(u):
        for j in ORDER + (0,):
            for e in range(2):
                if j + e:
                    second_to(u, j, e).start()
        second_self(u).start()

    def second_sent(u):
        for j in ORDER + (0,):
            for e in range(2):
                if j + e:
                    second_to(u, j, e).wait_send()

    def first_sent(b, ch):
        for j in ORDER:
            first_copy(b, ch, j, m, mom_to(j), mom_to(j)).wait_send()

    def first_arrived(b):
        def step(ch, carry):
            for j in range(1, 8):
                first_copy(b, ch, j, mom_from(j), m, mom_to(j)).wait_recv()
            first_self(b, ch).wait()
            return carry

        lax.fori_loop(0, 4, step, 0)

    def transform_block(b):
        for nu in range(2):

            def transform(half, carry, nu=nu):
                cols = pl.ds(aligned(half * 256, 256), 256)
                spec = dot(fwd[...], recv1[b, nu, :, cols])
                real, imag = spec[:256], spec[256:]

                def weight(ri):
                    return jnp.concatenate(
                        [w32[pl.ds(ri * 2048 + (2 * half + t) * 2 + nu, 256, stride=8), :] for t in range(2)],
                        axis=1,
                    )

                wr, wi = weight(0), weight(1)
                prod = jnp.concatenate([wr * real - wi * imag, wr * imag + wi * real], axis=0)
                back = dot(inv[...], prod.astype(BF16)).reshape(16, 4, 8, 256)
                send2[b, :, :, 8 * nu : 8 * nu + 8, cols] = back.astype(BF16)
                return carry

            lax.fori_loop(0, 2, transform, 0)

    def resend(ch, carry):
        first_sent(0, ch)
        send_first(1, ch)
        return carry

    lax.fori_loop(0, 4, resend, 0)
    first_arrived(0)
    transform_block(0)
    first_sent(1, 0)
    first_sent(1, 1)
    send_second(0)
    first_sent(1, 2)
    first_sent(1, 3)
    send_second(1)
    first_arrived(1)
    transform_block(1)
    second_sent(0)
    send_second(2)
    share_c.wait_send()
    remote(c.at[:, half], c_both.at[:, :, points_other], s0, r0, (m, p_other)).wait_recv()

    def second_arrived(u):
        for j in range(8):
            for e in range(2):
                if j + e:
                    second_from(u, j, e).wait_recv()
        second_self(u).wait()

    def momenta(u):
        return 4 * UNITS[u][2]

    def band_unit(u):
        b, first, n = UNITS[u]
        for i in range(n):
            for t in range(4):
                spread[t, 256 * i : 256 * (i + 1), :] = (
                    recv2[b, first + i, :, :, 128 * t : 128 * (t + 1)].astype(F32).reshape(256, 128)
                )
        mixed = []
        for i in range(4 * n):
            rows = [
                jnp.concatenate(
                    [
                        spread.at[t][pl.ds((i // 4) * 256 + ri * 4 + i % 4, 32, stride=8), :]
                        for t in range(4)
                    ],
                    axis=1,
                )
                for ri in range(2)
            ]
            k = 16 * pc + 4 * first + i
            vk = jnp.concatenate([v[0, k], v[1, k]], axis=0)
            mixed.append(dot(jnp.concatenate(rows, axis=0).astype(BF16), vk, NT))
        lefts = []
        for o in mixed:
            q = o[:32] + sign * pltpu.roll(o[32:], 64, 1)
            lefts.append(jnp.concatenate([q, pltpu.roll(q, 64, 1) * -sign], axis=0).astype(BF16))
        for i, left in enumerate(lefts):
            ck = jnp.concatenate([c_both[0, 4 * first + i], c_both[1, 4 * first + i]], axis=0)
            band[u][pl.ds(i, 128, stride=4 * n), :] = dot(left, ck, TN)

    def y_copy(u, d):
        i = u * 3 + d - 1
        return remote(send_y[u].at[d - 1], recv_y[u].at[d - 1], sy.at[i], ry.at[i], y_to(d))

    def z_copy(u, d):
        i = u * 3 + d - 1
        return remote(send_z[u].at[d - 1], recv_z[u].at[d - 1], sz.at[i], rz.at[i], z_to(d))

    def y_start(u):
        k = momenta(u)
        for d in (2, 1, 3):
            for ri in range(2):
                row = aligned((ri * 4 + (py + d) % 4) * 16 * k, 16 * k)
                send_y[u][d - 1, ri] = band[u][pl.ds(row, 16 * k), :].astype(BF16)
            y_copy(u, d).start()

    def z_start(u):
        k = momenta(u)
        for d in range(1, 4):
            y_copy(u, d).wait_recv()
        for d in (2, 1, 3, 0):
            zz = aligned(((ph + d) % 4) * 4 * k, 4 * k)
            for ri in range(2):
                part = band[u][pl.ds(aligned((ri * 4 + py) * 16 * k + zz, 4 * k), 4 * k), :]
                for i in range(3):
                    part += recv_y[u][i, ri, pl.ds(zz, 4 * k), :].astype(F32)
                if d == 0:
                    own_z[u][ri] = part
                else:
                    send_z[u][d - 1, ri] = part.astype(BF16)
            if d:
                z_copy(u, d).start()

    def swap_to(u, e):
        i = u * 2 + e
        return remote(send_p[u].at[e], recv_p[u].at[pc], sp.at[i], rp.at[i], ((m + 4) % 8, pts_of(e)))

    def swap_from(u, e):
        i = u * 2 + e
        return remote(send_p[u].at[e], recv_p[u].at[core_of(e)], sp.at[i], rp.at[i], ((m + 4) % 8, pts_of(e)))

    def core_copy(u):
        return remote(total[u].at[:, 1 - pc], peer_total[u], st.at[u], rt.at[u], (m, p_other))

    def finish(u):
        k = momenta(u)
        for d in range(1, 4):
            z_copy(u, d).wait_recv()
        for ri in range(2):
            part = own_z[u][ri]
            for i in range(3):
                part += recv_z[u][i, ri].astype(F32)
            total[u][ri] = part.reshape(2, 2 * k, 128)
        swap_start(u)

    def wide_copy(u, d, e, t, source):
        i = ((u - 3) * 2 + t) * 8 + e * 4 + d
        return remote(
            send_w.at[u - 3, d, core_of(e)], recv_w.at[u - 3, t, source, d], sw.at[i], rw.at[i], wide_to(d, e, t)
        )

    def wide_start(u):
        for d in range(1, 4):
            y_copy(u, d).wait_recv()
        for d in (2, 1, 3, 0):
            zz = aligned(((ph + d) % 4) * 16, 16)
            for ri in range(2):
                part = band[u][pl.ds(aligned((ri * 4 + py) * 64 + zz, 16), 16), :]
                for i in range(3):
                    part += recv_y[u][i, ri, pl.ds(zz, 16), :].astype(F32)
                if d == 0:
                    total[u][ri] = part.reshape(2, 8, 128)
                for core in range(2):
                    send_w[u - 3, d, core, 8 * ri : 8 * ri + 8, :] = part[8 * core : 8 * core + 8].astype(BF16)
            for dd, e, t in WIDE:
                if dd == d:
                    wide_copy(u, d, e, t, pc).start()
        recv_w[u - 3, 0, pc, 0] = jnp.zeros((16, 128), BF16)

    def wide_place(u):
        b, first, _ = UNITS[u]
        for d, e, t in WIDE:
            wide_copy(u, d, e, t, core_of(e)).wait_recv()
        for core in range(2):
            here, there = [sum(recv_w[u - 3, t, core, d].astype(F32) for d in range(4)) for t in range(2)]
            for ri in range(2):
                for row in range(2):
                    part = slice(8 * ri + 4 * row, 8 * ri + 4 * row + 4)
                    top = 16 * core + 4 * first
                    mirror[b, ri, row, top : top + 4, :] = there[part]
                    rows = out_rows(b, ri, row, top, 4)
                    before = out[rows, :]
                    out[rows, :] = before + here[part] if b else before - here[part]
        for ri in range(2):
            own = total[u][ri, pc]
            for row in range(2):
                part = own[4 * row : 4 * row + 4]
                rows = out_rows(b, ri, row, 16 * pc + 4 * first, 4)
                before = out[rows, :]
                out[rows, :] = before + part if b else before - part

    def swap_start(u):
        k = momenta(u)
        for e in range(2):
            for ri in range(2):
                send_p[u][e, 2 * k * ri : 2 * k * (ri + 1), :] = total[u][ri, core_of(e)].astype(BF16)
            swap_to(u, e).start()
        core_copy(u).start()

    def y_sent(u):
        for d in range(1, 4):
            y_copy(u, d).wait_send()

    def z_sent(u):
        for d in range(1, 4):
            z_copy(u, d).wait_send()

    def swap_sent(u):
        core_copy(u).wait_send()
        for e in range(2):
            swap_to(u, e).wait_send()

    def out_rows(b, ri, row, first, count):
        return pl.ds((ri * 2 + b) * 64 + row + 2 * first, count, stride=2)

    def own_term():
        for row in range(2):
            energy = jnp.sum(jnp.where(slot == across, val_e[row : row + 1, :], 0.0), axis=1, keepdims=True)
            gap = cond_e[...] - energy
            for b in range(2):
                for ri in range(2):
                    rows = pl.ds((ri * 2 + b) * 512 + 2 * (p % 8) + row, 32, stride=16)
                    result = gap * own_x[rows, :]
                    out[out_rows(b, ri, row, 0, 32), :] = -result if b else result

    def place(u):
        b, first, n = UNITS[u]
        k = 4 * n
        for e in range(2):
            swap_from(u, e).wait_recv()
        for core in range(2):
            turned = recv_p[u][core].astype(F32)
            for ri in range(2):
                for row in range(2):
                    top = (2 * ri + row) * k
                    mirror[b, ri, row, 16 * core + 4 * first : 16 * core + 4 * first + k, :] = turned[top : top + k]
        core_copy(u).wait_recv()
        for ri in range(2):
            for row in range(2):
                for e in range(2):
                    part = peer_total[u][ri] if e else total[u][ri, pc]
                    part = part[k * row : k * (row + 1)]
                    rows = out_rows(b, ri, row, 16 * core_of(e) + 4 * first, k)
                    before = out[rows, :]
                    out[rows, :] = before + part if b else before - part

    def add_mirrored(b):
        for row in range(2):
            for ri in range(2):
                mirrored = dot(pick, mirror[b, ri, row].astype(BF16), TN)
                rows = out_rows(1 - b, ri, row, 0, 32)
                before = out[rows, :]
                out[rows, :] = before - mirrored if b != ri else before + mirrored

    slot = lax.broadcasted_iota(jnp.int32, (32, 32), 0)
    across = lax.broadcasted_iota(jnp.int32, (32, 32), 1)
    pick = jnp.where(slot == (opp_row[...] & 31), 1.0, 0.0).astype(BF16)
    own_term()
    second_arrived(0)
    band_unit(0)
    y_start(0)
    second_sent(1)
    send_second(3)
    second_arrived(1)
    band_unit(1)
    y_start(1)
    z_start(0)
    second_sent(2)
    send_second(4)
    second_arrived(2)
    band_unit(2)
    y_start(2)
    z_start(1)
    finish(0)
    second_arrived(3)
    band_unit(3)
    y_start(3)
    z_start(2)
    finish(1)
    second_arrived(4)
    band_unit(4)
    y_start(4)
    wide_start(3)
    finish(2)
    place(0)
    place(1)
    wide_start(4)
    add_mirrored(0)
    second_sent(3)
    second_sent(4)
    place(2)
    for u in range(5):
        y_sent(u)
    for u in range(3):
        z_sent(u)
        swap_sent(u)
    wide_place(3)
    wide_place(4)
    add_mirrored(1)
    for u in (3, 4):
        for d, e, t in WIDE:
            wide_copy(u, d, e, t, pc).wait_send()


def on_device(
    amplitudes, val_orbitals, cond_orbitals, screened, val_energy, cond_energy, grid_of_slot, opposite_slot
):
    weights = screened.reshape(2, 256, 2, 4, 128).transpose(0, 1, 3, 2, 4).reshape(4096, 128)
    hbm = pl.BlockSpec(memory_space=pl.ANY)
    vmem = pl.BlockSpec(memory_space=pltpu.VMEM)
    dma = pltpu.SemaphoreType.DMA

    def each(shape):
        return tuple(shape(4 * n) for _, _, n in UNITS)

    out = pl.pallas_call(
        kernel,
        out_shape=pltpu.VMEM((256, 128), F32),
        in_specs=[hbm] * 4 + [vmem] * 4,
        out_specs=vmem,
        scratch_shapes=[
            pltpu.VMEM((2, 2, 32, 64, 128), BF16),
            pltpu.VMEM((2, 32, 64, 512), BF16),
            pltpu.VMEM((2, 32, 16, 128), BF16),
            pltpu.VMEM((2, 16, 32, 128), BF16),
            pltpu.VMEM((4096, 128), BF16),
            pltpu.VMEM((4096, 128), F32),
            pltpu.VMEM((512, 512), BF16),
            pltpu.VMEM((512, 512), BF16),
            pltpu.VMEM((4, 512, 128), F32),
            pltpu.VMEM((2, 4, 16, 16, 512), BF16),
            pltpu.VMEM((2, 2, 512, 512), BF16),
            pltpu.VMEM((2, 16, 4, 16, 512), BF16),
            pltpu.VMEM((2, 4, 16, 16, 512), BF16),
            each(lambda k: pltpu.VMEM((128 * k, 128), F32)),
            pltpu.VMEM((2048, 128), F32),
            each(lambda k: pltpu.VMEM((3, 2, 16 * k, 128), BF16)),
            each(lambda k: pltpu.VMEM((3, 2, 16 * k, 128), BF16)),
            each(lambda k: pltpu.VMEM((2, 4 * k, 128), F32)),
            each(lambda k: pltpu.VMEM((3, 2, 4 * k, 128), BF16)),
            each(lambda k: pltpu.VMEM((3, 2, 4 * k, 128), BF16)),
            pltpu.VMEM((2, 4, 2, 16, 128), BF16),
            pltpu.VMEM((2, 2, 2, 4, 16, 128), BF16),
            each(lambda k: pltpu.VMEM((2, 2, 2 * k, 128), F32)),
            each(lambda k: pltpu.VMEM((2, 2 * k, 128), F32)),
            each(lambda k: pltpu.VMEM((2, 4 * k, 128), BF16)),
            each(lambda k: pltpu.VMEM((2, 4 * k, 128), BF16)),
            pltpu.VMEM((2, 2, 2, 32, 128), F32),
            dma((10,)), dma((13,)), dma, dma, dma((64,)), dma((64,)), dma((80,)), dma((80,)),
            dma((15,)), dma((15,)), dma((15,)), dma((15,)), dma((32,)), dma((32,)), dma((10,)), dma((10,)), dma((5,)), dma((5,)),
        ],
        compiler_params=pltpu.CompilerParams(
            collective_id=0, has_side_effects=True, vmem_limit_bytes=56 * 2**20
        ),
        cost_estimate=pl.CostEstimate(flops=2800000000, bytes_accessed=8000000, transcendentals=131072),
    )(
        amplitudes.reshape(2, 2, 32, 64, 128),
        val_orbitals,
        cond_orbitals,
        weights,
        val_energy.T,
        cond_energy,
        grid_of_slot.reshape(1, 256),
        opposite_slot.reshape(1, 32),
    )
    return out.reshape(2, 2, 1, 32, 2, 128)


def solution(mesh):
    in_specs = (
        P(None, None, None, "mom", None, None),
        P(None, "mom", None, None),
        P(None, "mom", "pts", None),
        P(None, None, ("pts", "mom"), None),
        P("mom", "pts"),
        P("mom", None),
        P(),
        P("mom"),
    )
    out_specs = P(None, None, None, "mom", "pts", None)
    return jax.shard_map(
        on_device, mesh=mesh, in_specs=in_specs, out_specs=out_specs, check_vma=False
    )
```

```python
import math

import jax
import jax.numpy as jnp
from jax import lax
from jax.experimental import pallas as pl
from jax.experimental.pallas import tpu as pltpu
from jax.sharding import PartitionSpec as P

MESH = pl.DeviceIdType.MESH
F32 = jnp.float32
BF16 = jnp.bfloat16
NT = (((1,), (1,)), ((), ()))
TN = (((0,), (0,)), ((), ()))
ORDER = (2, 6, 1, 5, 3, 7, 4)
WIDE = tuple((d, e, t) for d in (2, 1, 3, 0) for t in (1, 0) for e in (0, 1) if d + e + t)
UNITS = ((0, 0, 2), (0, 2, 2), (1, 0, 2), (1, 2, 1), (1, 3, 1))


def dot(a, b, dims=(((1,), (0,)), ((), ()))):
    return lax.dot_general(a, b, dims, preferred_element_type=F32)


def aligned(value, by):
    return pl.multiple_of(value, by)


def kernel(
    x_hbm, v_hbm, c_hbm, w_hbm, val_e, cond_e, grid_row, opp_row,
    out,
    x, v, c, c_both, w, w32, fwd, inv, spread, send1, recv1, send2, recv2, band, own_x,
    send_y, recv_y, own_z, send_z, recv_z, send_w, recv_w, total, peer_total,
    send_p, recv_p, mirror,
    load_sem, self_sem, s0, r0, s1, r1, s2, r2, sy, ry, sz, rz, sw, rw, sp, rp, st, rt,
):
    m = lax.axis_index("mom")
    p = lax.axis_index("pts")
    mx, mz = m % 4, m // 4
    py, ph, pc = p // 8, (p // 2) % 4, p % 2
    p_other = p + 1 - 2 * pc

    def mom_to(j):
        return ((mz + j // 4) % 2) * 4 + (mx + j % 4) % 4

    def mom_from(j):
        return ((mz + j // 4) % 2) * 4 + (mx + 4 - j % 4) % 4

    def pts_of(e):
        return p_other if e else p

    def core_of(e):
        return 1 - pc if e else pc

    def y_to(d):
        return (m, ((py + d) % 4) * 8 + p % 8)

    def z_to(d):
        return (m, py * 8 + ((ph + d) % 4) * 2 + pc)

    def wide_to(d, e, t):
        return ((m + 4 * t) % 8, py * 8 + ((ph + d) % 4) * 2 + core_of(e))

    def remote(src, dst, send, recv, peer):
        return pltpu.make_async_remote_copy(
            src_ref=src, dst_ref=dst, send_sem=send, recv_sem=recv, device_id=peer, device_id_type=MESH
        )

    def load_x(ch):
        rows = pl.ds(8 * ch, 8)
        return pltpu.make_async_copy(x_hbm.at[:, :, rows], x.at[:, :, rows], load_sem.at[ch])

    def load_v(ch):
        rows = pl.ds(8 * ch, 8)
        return pltpu.make_async_copy(v_hbm.at[:, rows], v.at[:, rows], load_sem.at[4 + ch])

    load_c = pltpu.make_async_copy(c_hbm, c, load_sem.at[8])
    load_w = pltpu.make_async_copy(w_hbm, w, load_sem.at[9])
    load_c.start()
    load_x(0).start()
    load_v(0).start()

    barrier = pltpu.get_barrier_semaphore()
    peers = [(mom_to(j), pts_of(e)) for j in range(8) for e in range(2) if j + e]
    peers += [y_to(d) for d in range(1, 4)] + [wide_to(d, e, t) for d, e, t in WIDE if d]
    for peer in peers:
        pl.semaphore_signal(barrier, inc=1, device_id=peer, device_id_type=MESH)

    lane = lax.broadcasted_iota(jnp.int32, (32, 128), 1)
    sign = jnp.where(lane < 64, -1.0, 1.0).astype(F32)

    def first_copy(b, ch, j, src_m, dst_m, peer):
        i = (b * 4 + ch) * 8 + j
        return remote(
            send1.at[b, ch, pl.ds(2 * dst_m, 2)],
            recv1.at[b, :, pl.ds(aligned((src_m * 4 + ch) * 16, 16), 16), :],
            s1.at[i],
            r1.at[i],
            (peer, p),
        )

    def first_self(b, ch):
        return pltpu.make_async_copy(
            send1.at[b, ch, pl.ds(2 * m, 2)],
            recv1.at[b, :, pl.ds(aligned((m * 4 + ch) * 16, 16), 16), :],
            self_sem.at[b * 4 + ch],
        )

    def send_first(b, ch):
        for j in ORDER:
            first_copy(b, ch, j, m, mom_to(j), mom_to(j)).start()
        first_self(b, ch).start()

    def pair_chunk(ch):
        for group in range(2):
            ks = [group * 4 + u for u in range(4)]
            halves = []
            for k8 in ks:
                k = ch * 8 + k8
                xk = jnp.concatenate([x[0, 0, k], x[1, 0, k], x[0, 1, k], x[1, 1, k]], axis=0)
                ck = jnp.concatenate([c[0, k], c[1, k]], axis=0)
                halves.append(dot(ck, xk, NT))
            lefts = []
            for h in halves:
                parts = []
                for b in range(2):
                    cols = h[:, 128 * b : 128 * (b + 1)]
                    q = cols[:16] + sign[:16] * pltpu.roll(cols[16:], 64, 1)
                    parts += [q, pltpu.roll(q, 64, 1) * -sign[:16]]
                lefts.append(jnp.concatenate(parts, axis=0).astype(BF16))
            for k8, left in zip(ks, lefts):
                k = ch * 8 + k8
                pair = dot(left, jnp.concatenate([v[0, k], v[1, k]], axis=0))
                for b in range(2):
                    for ri in range(2):
                        top = (b * 2 + ri) * 16
                        for q in range(4):
                            spread.at[q][pl.ds(b * 256 + ri * 8 + k8, 16, stride=16), :] = pair[
                                top : top + 16, 128 * q : 128 * (q + 1)
                            ]

    def pack(b, ch):
        for q in range(4):
            send1[b, ch, :, :, 128 * q : 128 * (q + 1)] = (
                spread[q, 256 * b : 256 * (b + 1), :].astype(BF16).reshape(16, 16, 128)
            )

    def pair_and_send(ch, carry):
        load_x(ch).wait()
        load_v(ch).wait()
        pair_chunk(ch)
        pack(0, ch)
        send_first(0, ch)
        pack(1, ch)
        return carry

    load_c.wait()
    load_x(0).wait()
    load_v(0).wait()
    for ch in range(1, 4):
        load_x(ch).start()
        load_v(ch).start()
    load_w.start()
    pair_chunk(0)
    pack(0, 0)
    pl.semaphore_wait(barrier, len(peers))
    send_first(0, 0)
    pack(1, 0)
    half = pl.ds(16 * (1 - pc), 16)
    points = pl.ds(aligned(16 * pc, 16), 16)
    points_other = pl.ds(aligned(16 * (1 - pc), 16), 16)
    share_c = remote(c.at[:, half], c_both.at[:, :, points], s0, r0, (m, p_other))
    share_c.start()
    lax.fori_loop(1, 4, pair_and_send, 0)
    c_both[:, :, points] = c[:, pl.ds(16 * pc, 16)]

    def make_tables():
        frequency = lax.broadcasted_iota(jnp.int32, (256, 256), 0)
        angle = ((frequency * grid_row[...]) & 255).astype(F32) * (2.0 * math.pi / 256)
        slot = lax.broadcasted_iota(jnp.int32, (256, 512), 0)
        column = lax.broadcasted_iota(jnp.int32, (256, 512), 1)
        cos_table = jnp.cos(angle).astype(BF16)
        sin_table = jnp.sin(angle).astype(BF16)

        def halves(slots, real):
            place = jnp.where(slot == slots, 1.0, 0.0).astype(BF16)
            cosine, sine = dot(cos_table, place), dot(sin_table, place)
            return jnp.where(real, cosine, sine), jnp.where(real, -sine, cosine)

        top, bottom = halves((column >> 4) * 8 + (column & 7), (column & 8) == 0)
        fwd[:256, :] = top.astype(BF16)
        fwd[256:, :] = bottom.astype(BF16)
        top, bottom = halves((column >> 5) * 16 + ((column >> 3) & 3) * 4 + (column & 3), (column & 4) == 0)
        inv[:, :256] = (top.T * (1.0 / 256)).astype(BF16)
        inv[:, 256:] = (bottom.T * (1.0 / 256)).astype(BF16)

    make_tables()
    first_row = aligned((p // 8) * 16, 16)
    for ri in range(2):
        for b in range(2):
            piece = x[ri, b, :, pl.ds(first_row, 16), :].astype(F32)
            own_x[pl.ds((ri * 2 + b) * 512, 512), :] = piece.reshape(512, 128)
    load_w.wait()
    w32[...] = w[...].astype(F32)

    def second_copy(u, j, e, src_m, src_c, dst_m, dst_c, peer):
        b, q, n = UNITS[u]
        i = (u * 8 + j) * 2 + e
        return remote(
            send2.at[b, dst_m * 2 + dst_c, pl.ds(q, n)],
            recv2.at[b, pl.ds(q, n), src_c * 8 + src_m],
            s2.at[i],
            r2.at[i],
            peer,
        )

    def second_to(u, j, e):
        return second_copy(u, j, e, m, pc, mom_to(j), core_of(e), (mom_to(j), pts_of(e)))

    def second_from(u, j, e):
        return second_copy(u, j, e, mom_from(j), core_of(e), m, pc, (mom_to(j), pts_of(e)))

    def second_self(u):
        b, q, n = UNITS[u]
        return pltpu.make_async_copy(
            send2.at[b, m * 2 + pc, pl.ds(q, n)], recv2.at[b, pl.ds(q, n), pc * 8 + m], self_sem.at[8 + u]
        )

    def send_second(u):
        for j in ORDER + (0,):
            for e in range(2):
                if j + e:
                    second_to(u, j, e).start()
        second_self(u).start()

    def second_sent(u):
        for j in ORDER + (0,):
            for e in range(2):
                if j + e:
                    second_to(u, j, e).wait_send()

    def first_sent(b, ch):
        for j in ORDER:
            first_copy(b, ch, j, m, mom_to(j), mom_to(j)).wait_send()

    def first_arrived(b):
        def step(ch, carry):
            for j in range(1, 8):
                first_copy(b, ch, j, mom_from(j), m, mom_to(j)).wait_recv()
            first_self(b, ch).wait()
            return carry

        lax.fori_loop(0, 4, step, 0)

    def transform_block(b):
        for nu in range(2):

            def transform(half, carry, nu=nu):
                cols = pl.ds(aligned(half * 256, 256), 256)
                spec = dot(fwd[...], recv1[b, nu, :, cols])
                real, imag = spec[:256], spec[256:]

                def weight(ri):
                    return jnp.concatenate(
                        [w32[pl.ds(ri * 2048 + (2 * half + t) * 2 + nu, 256, stride=8), :] for t in range(2)],
                        axis=1,
                    )

                wr, wi = weight(0), weight(1)
                prod = jnp.concatenate([wr * real - wi * imag, wr * imag + wi * real], axis=0)
                back = dot(inv[...], prod.astype(BF16)).reshape(16, 4, 8, 256)
                send2[b, :, :, 8 * nu : 8 * nu + 8, cols] = back.astype(BF16)
                return carry

            lax.fori_loop(0, 2, transform, 0)

    def resend(ch, carry):
        first_sent(0, ch)
        send_first(1, ch)
        return carry

    lax.fori_loop(0, 4, resend, 0)
    first_arrived(0)
    transform_block(0)
    first_sent(1, 0)
    first_sent(1, 1)
    send_second(0)
    first_sent(1, 2)
    first_sent(1, 3)
    send_second(1)
    first_arrived(1)
    transform_block(1)
    second_sent(0)
    send_second(2)
    share_c.wait_send()
    remote(c.at[:, half], c_both.at[:, :, points_other], s0, r0, (m, p_other)).wait_recv()

    def second_arrived(u):
        for j in range(8):
            for e in range(2):
                if j + e:
                    second_from(u, j, e).wait_recv()
        second_self(u).wait()

    def momenta(u):
        return 4 * UNITS[u][2]

    def band_unit(u):
        b, first, n = UNITS[u]
        for i in range(n):
            for t in range(4):
                spread[t, 256 * i : 256 * (i + 1), :] = (
                    recv2[b, first + i, :, :, 128 * t : 128 * (t + 1)].astype(F32).reshape(256, 128)
                )
        mixed = []
        for i in range(4 * n):
            rows = [
                jnp.concatenate(
                    [
                        spread.at[t][pl.ds((i // 4) * 256 + ri * 4 + i % 4, 32, stride=8), :]
                        for t in range(4)
                    ],
                    axis=1,
                )
                for ri in range(2)
            ]
            k = 16 * pc + 4 * first + i
            vk = jnp.concatenate([v[0, k], v[1, k]], axis=0)
            mixed.append(dot(jnp.concatenate(rows, axis=0).astype(BF16), vk, NT))
        lefts = []
        for o in mixed:
            q = o[:32] + sign * pltpu.roll(o[32:], 64, 1)
            lefts.append(jnp.concatenate([q, pltpu.roll(q, 64, 1) * -sign], axis=0).astype(BF16))
        for i, left in enumerate(lefts):
            ck = jnp.concatenate([c_both[0, 4 * first + i], c_both[1, 4 * first + i]], axis=0)
            band[u][pl.ds(i, 128, stride=4 * n), :] = dot(left, ck, TN)

    def y_copy(u, d):
        i = u * 3 + d - 1
        return remote(send_y[u].at[d - 1], recv_y[u].at[d - 1], sy.at[i], ry.at[i], y_to(d))

    way = 1 - 2 * pc

    def z_place(steps):
        return (ph + way * steps + 8) % 4

    def z_copy(u, d):
        i = u * 3 + d - 1
        peer = z_to(d)
        if u < 2:
            peer = (m, py * 8 + z_place(-1 if d == 2 else 1) * 2 + pc)
        return remote(send_z[u].at[d - 1], recv_z[u].at[d - 1], sz.at[i], rz.at[i], peer)

    def z_part(u, ri, place):
        k = momenta(u)
        zz = aligned(place * 4 * k, 4 * k)
        part = band[u][pl.ds(aligned((ri * 4 + py) * 16 * k + zz, 4 * k), 4 * k), :]
        for i in range(3):
            part += recv_y[u][i, ri, pl.ds(zz, 4 * k), :].astype(F32)
        return part

    def relay_start(u):
        for d in range(1, 4):
            y_copy(u, d).wait_recv()
        for d, steps in ((1, 2), (2, -1)):
            for ri in range(2):
                send_z[u][d - 1, ri] = z_part(u, ri, z_place(steps)).astype(BF16)
            z_copy(u, d).start()
        for ri in range(2):
            own_z[u][ri] = z_part(u, ri, ph)

    def relay_pass(u):
        z_copy(u, 1).wait_recv()
        for ri in range(2):
            send_z[u][2, ri] = (z_part(u, ri, z_place(1)) + recv_z[u][0, ri].astype(F32)).astype(BF16)
        z_copy(u, 3).start()

    def y_start(u):
        k = momenta(u)
        for d in (2, 1, 3):
            for ri in range(2):
                row = aligned((ri * 4 + (py + d) % 4) * 16 * k, 16 * k)
                send_y[u][d - 1, ri] = band[u][pl.ds(row, 16 * k), :].astype(BF16)
            y_copy(u, d).start()

    def z_start(u):
        k = momenta(u)
        for d in range(1, 4):
            y_copy(u, d).wait_recv()
        for d in (2, 1, 3, 0):
            zz = aligned(((ph + d) % 4) * 4 * k, 4 * k)
            for ri in range(2):
                part = band[u][pl.ds(aligned((ri * 4 + py) * 16 * k + zz, 4 * k), 4 * k), :]
                for i in range(3):
                    part += recv_y[u][i, ri, pl.ds(zz, 4 * k), :].astype(F32)
                if d == 0:
                    own_z[u][ri] = part
                else:
                    send_z[u][d - 1, ri] = part.astype(BF16)
            if d:
                z_copy(u, d).start()

    def swap_to(u, e):
        i = u * 2 + e
        return remote(send_p[u].at[e], recv_p[u].at[pc], sp.at[i], rp.at[i], ((m + 4) % 8, pts_of(e)))

    def swap_from(u, e):
        i = u * 2 + e
        return remote(send_p[u].at[e], recv_p[u].at[core_of(e)], sp.at[i], rp.at[i], ((m + 4) % 8, pts_of(e)))

    def core_copy(u):
        return remote(total[u].at[:, 1 - pc], peer_total[u], st.at[u], rt.at[u], (m, p_other))

    def finish(u):
        k = momenta(u)
        slots = (1, 2) if u < 2 else (0, 1, 2)
        for i in slots:
            z_copy(u, i + 1).wait_recv()
        for ri in range(2):
            part = own_z[u][ri]
            for i in slots:
                part += recv_z[u][i, ri].astype(F32)
            total[u][ri] = part.reshape(2, 2 * k, 128)
        swap_start(u)

    def wide_copy(u, d, e, t, source):
        i = ((u - 3) * 2 + t) * 8 + e * 4 + d
        return remote(
            send_w.at[u - 3, d, core_of(e)], recv_w.at[u - 3, t, source, d], sw.at[i], rw.at[i], wide_to(d, e, t)
        )

    def wide_start(u):
        for d in range(1, 4):
            y_copy(u, d).wait_recv()
        for d in (2, 1, 3, 0):
            zz = aligned(((ph + d) % 4) * 16, 16)
            for ri in range(2):
                part = band[u][pl.ds(aligned((ri * 4 + py) * 64 + zz, 16), 16), :]
                for i in range(3):
                    part += recv_y[u][i, ri, pl.ds(zz, 16), :].astype(F32)
                if d == 0:
                    total[u][ri] = part.reshape(2, 8, 128)
                for core in range(2):
                    send_w[u - 3, d, core, 8 * ri : 8 * ri + 8, :] = part[8 * core : 8 * core + 8].astype(BF16)
            for dd, e, t in WIDE:
                if dd == d:
                    wide_copy(u, d, e, t, pc).start()
        recv_w[u - 3, 0, pc, 0] = jnp.zeros((16, 128), BF16)

    def wide_place(u):
        b, first, _ = UNITS[u]
        for d, e, t in WIDE:
            wide_copy(u, d, e, t, core_of(e)).wait_recv()
        for core in range(2):
            here, there = [sum(recv_w[u - 3, t, core, d].astype(F32) for d in range(4)) for t in range(2)]
            for ri in range(2):
                for row in range(2):
                    part = slice(8 * ri + 4 * row, 8 * ri + 4 * row + 4)
                    top = 16 * core + 4 * first
                    mirror[b, ri, row, top : top + 4, :] = there[part]
                    rows = out_rows(b, ri, row, top, 4)
                    before = out[rows, :]
                    out[rows, :] = before + here[part] if b else before - here[part]
        for ri in range(2):
            own = total[u][ri, pc]
            for row in range(2):
                part = own[4 * row : 4 * row + 4]
                rows = out_rows(b, ri, row, 16 * pc + 4 * first, 4)
                before = out[rows, :]
                out[rows, :] = before + part if b else before - part

    def swap_start(u):
        k = momenta(u)
        for e in range(2):
            for ri in range(2):
                send_p[u][e, 2 * k * ri : 2 * k * (ri + 1), :] = total[u][ri, core_of(e)].astype(BF16)
            swap_to(u, e).start()
        core_copy(u).start()

    def y_sent(u):
        for d in range(1, 4):
            y_copy(u, d).wait_send()

    def z_sent(u):
        for d in range(1, 4):
            z_copy(u, d).wait_send()

    def swap_sent(u):
        core_copy(u).wait_send()
        for e in range(2):
            swap_to(u, e).wait_send()

    def out_rows(b, ri, row, first, count):
        return pl.ds((ri * 2 + b) * 64 + row + 2 * first, count, stride=2)

    def own_term():
        for row in range(2):
            energy = jnp.sum(jnp.where(slot == across, val_e[row : row + 1, :], 0.0), axis=1, keepdims=True)
            gap = cond_e[...] - energy
            for b in range(2):
                for ri in range(2):
                    rows = pl.ds((ri * 2 + b) * 512 + 2 * (p % 8) + row, 32, stride=16)
                    result = gap * own_x[rows, :]
                    out[out_rows(b, ri, row, 0, 32), :] = -result if b else result

    def place(u):
        b, first, n = UNITS[u]
        k = 4 * n
        for e in range(2):
            swap_from(u, e).wait_recv()
        for core in range(2):
            turned = recv_p[u][core].astype(F32)
            for ri in range(2):
                for row in range(2):
                    top = (2 * ri + row) * k
                    mirror[b, ri, row, 16 * core + 4 * first : 16 * core + 4 * first + k, :] = turned[top : top + k]
        core_copy(u).wait_recv()
        for ri in range(2):
            for row in range(2):
                for e in range(2):
                    part = peer_total[u][ri] if e else total[u][ri, pc]
                    part = part[k * row : k * (row + 1)]
                    rows = out_rows(b, ri, row, 16 * core_of(e) + 4 * first, k)
                    before = out[rows, :]
                    out[rows, :] = before + part if b else before - part

    def add_mirrored(b):
        for row in range(2):
            for ri in range(2):
                mirrored = dot(pick, mirror[b, ri, row].astype(BF16), TN)
                rows = out_rows(1 - b, ri, row, 0, 32)
                before = out[rows, :]
                out[rows, :] = before - mirrored if b != ri else before + mirrored

    slot = lax.broadcasted_iota(jnp.int32, (32, 32), 0)
    across = lax.broadcasted_iota(jnp.int32, (32, 32), 1)
    pick = jnp.where(slot == (opp_row[...] & 31), 1.0, 0.0).astype(BF16)
    own_term()
    second_arrived(0)
    band_unit(0)
    y_start(0)
    second_sent(1)
    send_second(3)
    second_arrived(1)
    band_unit(1)
    y_start(1)
    relay_start(0)
    second_sent(2)
    send_second(4)
    second_arrived(2)
    band_unit(2)
    y_start(2)
    relay_start(1)
    relay_pass(0)
    second_arrived(3)
    band_unit(3)
    y_start(3)
    z_start(2)
    finish(0)
    relay_pass(1)
    second_arrived(4)
    band_unit(4)
    y_start(4)
    wide_start(3)
    finish(1)
    finish(2)
    place(0)
    wide_start(4)
    place(1)
    add_mirrored(0)
    second_sent(3)
    second_sent(4)
    place(2)
    for u in range(5):
        y_sent(u)
    for u in range(3):
        z_sent(u)
        swap_sent(u)
    wide_place(3)
    wide_place(4)
    add_mirrored(1)
    for u in (3, 4):
        for d, e, t in WIDE:
            wide_copy(u, d, e, t, pc).wait_send()


def on_device(
    amplitudes, val_orbitals, cond_orbitals, screened, val_energy, cond_energy, grid_of_slot, opposite_slot
):
    weights = screened.reshape(2, 256, 2, 4, 128).transpose(0, 1, 3, 2, 4).reshape(4096, 128)
    hbm = pl.BlockSpec(memory_space=pl.ANY)
    vmem = pl.BlockSpec(memory_space=pltpu.VMEM)
    dma = pltpu.SemaphoreType.DMA

    def each(shape):
        return tuple(shape(4 * n) for _, _, n in UNITS)

    out = pl.pallas_call(
        kernel,
        out_shape=pltpu.VMEM((256, 128), F32),
        in_specs=[hbm] * 4 + [vmem] * 4,
        out_specs=vmem,
        scratch_shapes=[
            pltpu.VMEM((2, 2, 32, 64, 128), BF16),
            pltpu.VMEM((2, 32, 64, 512), BF16),
            pltpu.VMEM((2, 32, 16, 128), BF16),
            pltpu.VMEM((2, 16, 32, 128), BF16),
            pltpu.VMEM((4096, 128), BF16),
            pltpu.VMEM((4096, 128), F32),
            pltpu.VMEM((512, 512), BF16),
            pltpu.VMEM((512, 512), BF16),
            pltpu.VMEM((4, 512, 128), F32),
            pltpu.VMEM((2, 4, 16, 16, 512), BF16),
            pltpu.VMEM((2, 2, 512, 512), BF16),
            pltpu.VMEM((2, 16, 4, 16, 512), BF16),
            pltpu.VMEM((2, 4, 16, 16, 512), BF16),
            each(lambda k: pltpu.VMEM((128 * k, 128), F32)),
            pltpu.VMEM((2048, 128), F32),
            each(lambda k: pltpu.VMEM((3, 2, 16 * k, 128), BF16)),
            each(lambda k: pltpu.VMEM((3, 2, 16 * k, 128), BF16)),
            each(lambda k: pltpu.VMEM((2, 4 * k, 128), F32)),
            each(lambda k: pltpu.VMEM((3, 2, 4 * k, 128), BF16)),
            each(lambda k: pltpu.VMEM((3, 2, 4 * k, 128), BF16)),
            pltpu.VMEM((2, 4, 2, 16, 128), BF16),
            pltpu.VMEM((2, 2, 2, 4, 16, 128), BF16),
            each(lambda k: pltpu.VMEM((2, 2, 2 * k, 128), F32)),
            each(lambda k: pltpu.VMEM((2, 2 * k, 128), F32)),
            each(lambda k: pltpu.VMEM((2, 4 * k, 128), BF16)),
            each(lambda k: pltpu.VMEM((2, 4 * k, 128), BF16)),
            pltpu.VMEM((2, 2, 2, 32, 128), F32),
            dma((10,)), dma((13,)), dma, dma, dma((64,)), dma((64,)), dma((80,)), dma((80,)),
            dma((15,)), dma((15,)), dma((15,)), dma((15,)), dma((32,)), dma((32,)), dma((10,)), dma((10,)), dma((5,)), dma((5,)),
        ],
        compiler_params=pltpu.CompilerParams(
            collective_id=0, has_side_effects=True, vmem_limit_bytes=56 * 2**20
        ),
        cost_estimate=pl.CostEstimate(flops=2800000000, bytes_accessed=8000000, transcendentals=131072),
    )(
        amplitudes.reshape(2, 2, 32, 64, 128),
        val_orbitals,
        cond_orbitals,
        weights,
        val_energy.T,
        cond_energy,
        grid_of_slot.reshape(1, 256),
        opposite_slot.reshape(1, 32),
    )
    return out.reshape(2, 2, 1, 32, 2, 128)


def solution(mesh):
    in_specs = (
        P(None, None, None, "mom", None, None),
        P(None, "mom", None, None),
        P(None, "mom", "pts", None),
        P(None, None, ("pts", "mom"), None),
        P("mom", "pts"),
        P("mom", None),
        P(),
        P("mom"),
    )
    out_specs = P(None, None, None, "mom", "pts", None)
    return jax.shard_map(
        on_device, mesh=mesh, in_specs=in_specs, out_specs=out_specs, check_vma=False
    )
```
